512 devices in a mesh: blk: 128 (over y_lo, x, z, core), tile: 4 (over y_hi).
Axes of the slice: x: 4, y: 8 (y_hi: 4, y_lo: 2; y = y_hi * 2 + y_lo), z: 8, core: 2. Of those that a mesh axis runs over, the one named last changes fastest.
Arguments:
- right_side: float32 [512, 512], P('blk', 'tile'), may hold values from -6 to 6
- points: float32 [3, 512, 512], P(None, 'blk', 'tile'), may hold values from -5 to 5
- basis: float32 [512, 512, 256], P('blk', 'tile'), may hold values from -0.125 to 0.125
- skeleton: float32 [128, 3, 256], P('blk'), may hold values from -5 to 5
- cluster_sizes: int32 [512], P('blk'), may hold values from 256 to 512, as said below
- near_list: int32 [512, 4], P('blk'), may hold values from 0 to 511, as said below
- near_count: int32 [512], P('blk'), may hold values from 1 to 4, as said below
- far_mask: int32 [128, 128], P('blk'), may hold values from 0 to 1, as said below
Outputs:
- solution: float32 [512, 512], P('blk', 'tile')
- residual: float32 [512, 512], P('blk', 'tile')
The draws below stay inside these ranges and needn't reach their ends.
Inputs may be any that keep to these rules, and one draw needn't show every extreme that they name: `cluster_sizes`: every leaf holds at least half of its slots live, and some leaf holds all 512. `near_list`: slot 0 names the leaf itself; every neighbour lies in the same subtree or in the subtree just before or after it in a closed loop of subtrees. `near_count`: some leaf uses all slots. `far_mask`: 0 or 1; 0 for a subtree with itself.
All inputs are finite; a program needn't handle non-finite values.
Results may differ from the reference program's by a relative error of at most 0.0003.
Values sent between devices are 32-bit elements; how exact they have to be, the bound alone decides.
A program may use at most 64 MiB of HBM per device.

```python
import math
import jax
import jax.numpy as jnp
from jax import lax

LEAF_DEV = 4
M = 512
K = 256
NEAR = 4
SUBTREES = 128
LEAVES = 512


def draw_cluster_sizes(key, part):
    key = jax.random.fold_in(key, 11)
    sizes = jax.random.randint(key, (LEAVES,), M // 2, M + 1)
    return sizes.at[0].set(M).astype(jnp.int32)


def draw_near_list(key, part):
    key = jax.random.fold_in(key, 12)
    key_any, key_low, key_high = jax.random.split(key, 3)
    rows = jnp.arange(LEAVES)
    group_start = rows // LEAF_DEV * LEAF_DEV
    base = group_start - LEAF_DEV
    offsets = jax.random.randint(key_any, (LEAVES, NEAR), 0, 3 * LEAF_DEV)
    ids = jnp.mod(base[:, None] + offsets, LEAVES)
    lower = jnp.mod(group_start - LEAF_DEV + jax.random.randint(key_low, (LEAVES,), 0, LEAF_DEV), LEAVES)
    upper = jnp.mod(group_start + LEAF_DEV + jax.random.randint(key_high, (LEAVES,), 0, LEAF_DEV), LEAVES)
    inside = rows - group_start
    ids = ids.at[:, 1].set(jnp.where(inside == 0, lower, ids[:, 1]))
    ids = ids.at[:, 2].set(jnp.where(inside == LEAF_DEV - 1, upper, ids[:, 2]))
    ids = ids.at[:, 0].set(rows)
    return ids.astype(jnp.int32)


def draw_near_count(key, part):
    key = jax.random.fold_in(key, 13)
    rows = jnp.arange(LEAVES)
    inside = rows % LEAF_DEV
    counts = jax.random.randint(key, (LEAVES,), 1, NEAR + 1)
    counts = jnp.where(inside == 0, jnp.maximum(counts, 2), counts)
    counts = jnp.where(inside == LEAF_DEV - 1, NEAR, counts)
    return counts.at[0].set(NEAR).astype(jnp.int32)


def draw_far_mask(key, part):
    key = jax.random.fold_in(key, 14)
    values = (jax.random.randint(key, (SUBTREES, SUBTREES), 0, 4) > 0).astype(jnp.int32)
    rows = jnp.arange(SUBTREES)
    same = rows[:, None] == rows[None, :]
    return jnp.where(same, 0, values).astype(jnp.int32)


def block_scale(stream_key, dims, pieces, low, top_value):
    level = 1.0
    for axis_at, blocks in pieces:
        heights = jax.random.uniform(jax.random.fold_in(jax.random.fold_in(stream_key, 6), axis_at), (blocks,), jnp.float32, low / len(pieces), top_value / len(pieces))
        level = level * jnp.repeat(jnp.exp(heights), dims[axis_at] // blocks).reshape((-1,) + (1,) * (len(dims) - 1 - axis_at))
    return level


def centred(key, extent, width, most, shards=(), held_as=jnp.bfloat16):
    drawn = jax.random.normal(key, extent, jnp.float32) * width
    if len(shards) > 0:
        drawn = block_scale(key, extent, shards, -0.22, 0.18) * drawn
    return jnp.clip(drawn, min=-most, max=most).astype(held_as)


def setup_inputs(seed: int = 0) -> dict:
    keys = jax.random.split(jax.random.key(seed), 9)
    right_side = centred(keys[0], (LEAVES, M), 1.0, 6.0, ((0, 128), (1, 4)), jnp.float32)
    points = centred(keys[1], (3, LEAVES, M), 1.0, 5.0, ((1, 128), (2, 4)), jnp.float32)
    basis = centred(keys[2], (LEAVES, M, K), (LEAF_DEV * M) ** -0.5, 0.125, ((0, 128), (1, 4)), jnp.float32)
    skeleton = centred(keys[3], (SUBTREES, 3, K), 1.0, 5.0, ((0, 128),), jnp.float32)
    cluster_sizes = draw_cluster_sizes(jax.random.fold_in(keys[8], 71), 0)
    near_list = draw_near_list(jax.random.fold_in(keys[8], 71), 0)
    near_count = draw_near_count(jax.random.fold_in(keys[8], 71), 0)
    far_mask = draw_far_mask(jax.random.fold_in(keys[8], 71), 0)
    return dict(right_side=right_side, points=points, basis=basis, skeleton=skeleton, cluster_sizes=cluster_sizes, near_list=near_list, near_count=near_count, far_mask=far_mask)


spread_sq = 0.25
exact_mode = lax.Precision.HIGHEST
norm_eps = 1e-06

def coupling(targets, sources):
    dist_sq = lax.optimization_barrier(jnp.sum((targets[:, :, None] - sources[:, None, :]) ** 2, axis=0))
    return 1.0 / jnp.sqrt(dist_sq + spread_sq)

def reference(right_side, points, basis, skeleton, cluster_sizes, near_list, near_count, far_mask):
    live = (jnp.arange(M)[None, :] < cluster_sizes[:, None]).astype(jnp.float32)
    near_scale = 2.0 / math.sqrt(M * NEAR)
    far_scale = 4.0 / math.sqrt(K * SUBTREES)
    slot_range = jnp.arange(NEAR)

    def apply_op(field):

        def near_one(leaf_id):
            neighbours = near_list[leaf_id]
            weights = (slot_range < near_count[leaf_id]).astype(jnp.float32)
            source_pts = points[:, neighbours, :]
            target_pts = points[:, leaf_id, :]
            blocks = jax.vmap(coupling, in_axes=(None, 1))(target_pts, source_pts)
            values = field[neighbours]
            images = jnp.einsum('jpq,jq->jp', blocks, values, precision=exact_mode)
            return lax.optimization_barrier(jnp.sum(images * weights[:, None], axis=0))
        near = lax.map(near_one, jnp.arange(LEAVES)) * near_scale
        coef = jnp.einsum('apk,ap->ak', basis, field, precision=exact_mode)
        coef = coef.reshape(SUBTREES, LEAF_DEV, K).sum(axis=1)
        mask_f = far_mask.astype(jnp.float32)

        def far_one(group):
            blocks = jax.vmap(coupling, in_axes=(None, 0))(skeleton[group], skeleton)
            terms = jnp.einsum('bik,bk->bi', blocks, coef, precision=exact_mode)
            return lax.optimization_barrier(jnp.sum(terms * mask_f[group][:, None], axis=0)) * far_scale
        sky = lax.map(far_one, jnp.arange(SUBTREES))
        sky_leaf = jnp.repeat(sky, LEAF_DEV, axis=0)
        far = jnp.einsum('apk,ak->ap', basis, sky_leaf, precision=exact_mode)
        return live * (field + near + far)
    start = live * right_side
    beta = jnp.sqrt(jnp.sum(start * start) + norm_eps)
    first = start / beta
    w_one = apply_op(first)
    h11 = jnp.sum(first * w_one)
    update = w_one - h11 * first
    h21 = jnp.sqrt(jnp.sum(update * update) + norm_eps)
    second = update / h21
    w_two = apply_op(second)
    h12 = jnp.sum(first * w_two)
    h22 = jnp.sum(second * w_two)
    rest = w_two - h12 * first - h22 * second
    h32 = jnp.sqrt(jnp.sum(rest * rest) + norm_eps)
    m_aa = h11 * h11 + h21 * h21
    m_ab = h11 * h12 + h21 * h22
    m_bb = h12 * h12 + h22 * h22 + h32 * h32
    determ = m_aa * m_bb - m_ab * m_ab
    y_one = beta * (m_bb * h11 - m_ab * h12) / determ
    y_two = beta * (m_aa * h12 - m_ab * h11) / determ
    solution = y_one * first + y_two * second
    residual = start - y_one * w_one - y_two * w_two
    return (solution, residual)
```

```python
import functools
import math

import jax
import jax.numpy as jnp
from jax import lax
from jax.experimental import pallas as pl
from jax.experimental.pallas import tpu as pltpu
from jax.sharding import PartitionSpec as P

MESH = pl.DeviceIdType.MESH
f32 = jnp.float32
spread_sq = 0.25
norm_eps = 1e-06

HALO_ONE, HALO_TWO, COEF_ONE, COEF_TWO, SKEL, FAR_ONE, FAR_TWO, SKY_ONE, SKY_TWO, SUM_TILE, SUM_BLK = range(11)
EXCHANGES = 11


def hops(step):
    dx, dyl, dz, dc = step
    return min(dx, 4 - dx) + dyl + min(dz, 8 - dz)


OTHERS = sorted(
    [(dx, dyl, dz, dc) for dx in range(4) for dyl in range(2) for dz in range(8) for dc in range(2) if dx or dyl or dz or dc],
    key=lambda step: -hops(step),
)


def kernel(
    rs_ref, pts_ref, basis_ref, skel_ref, sizes_ref, near_ref, count_ref, mask_ref,
    sol_ref, res_ref,
    hal1, hal2, abuf, skb, cbuf, pbuf, rtile, rblk,
    gfar, gnear, tfar, tnear, fcol, live_col, acc_near,
    ssem, rsem,
):
    g = lax.axis_index("blk")
    t = lax.axis_index("tile")
    near_scale = 2.0 / math.sqrt(512 * 4)
    far_scale = 4.0 / math.sqrt(256 * 128)

    core, z, x, yl = lax.rem(g, 2), lax.rem(g // 2, 8), lax.rem(g // 16, 4), g // 64
    low = {(dz, dc): lax.rem(z + dz, 8) * 2 + lax.rem(core + dc, 2) for dz in range(8) for dc in range(2)}
    high = {(dx, dy): lax.rem(yl + dy, 2) * 64 + lax.rem(x + dx, 4) * 16 for dx in range(4) for dy in range(2)}
    others = [high[s[0], s[1]] + low[s[2], s[3]] for s in OTHERS]
    tiles = [lax.rem(t + d, 4) for d in (2, 1, 3)]
    left, right = lax.rem(g + 127, 128), lax.rem(g + 1, 128)

    barrier = pltpu.get_barrier_semaphore()
    for tt in tiles:
        for gg in (left, right, g):
            pl.semaphore_signal(barrier, inc=1, device_id=(gg, tt), device_id_type=MESH)
    for gg in others:
        pl.semaphore_signal(barrier, inc=1, device_id=(gg, t), device_id_type=MESH)

    col = lax.broadcasted_iota(jnp.int32, (1, 128), 1) + t * 128
    live_row = jnp.concatenate([(col < sizes_ref[a]).astype(f32) for a in range(4)], axis=0)
    s_row = live_row * rs_ref[...]
    own_half = lax.rem(t, 2)
    goal_half = t // 2
    skel = skel_ref[0]
    sk_lo, sk_hi = skel[:, :128], skel[:, 128:]
    goals = jnp.where(goal_half == 0, sk_lo, sk_hi)
    sources = jnp.where(own_half == 0, sk_lo, sk_hi)
    skb[g] = jnp.concatenate([sources, jnp.zeros((1, 128), f32)], axis=0)
    for a in range(4):
        hal1[4 + t, a] = jnp.concatenate([pts_ref[c, a : a + 1, :] for c in range(3)] + [s_row[a : a + 1]], axis=0)
    stacked = jnp.concatenate(
        [s_row, live_row] + [pts_ref[c] for c in range(3)] + [goals, jnp.zeros((128 - 23, 128), f32)], axis=0
    )
    cols = stacked.T
    lane = lax.broadcasted_iota(jnp.int32, (128, 128), 1)

    def spread(i):
        return jnp.broadcast_to(cols[:, i : i + 1], (128, 128))

    part_lo = jnp.zeros((128, 128), f32)
    part_hi = jnp.zeros((128, 128), f32)
    for a in range(4):
        s_b = spread(a)
        fcol[a] = s_b
        live_col[a] = spread(4 + a)
        part_lo = part_lo + basis_ref[a, :, :128] * s_b
        part_hi = part_hi + basis_ref[a, :, 128:] * s_b
    abuf[0, t, 0:1] = jnp.sum(part_lo, axis=0, keepdims=True)
    abuf[0, t, 1:2] = jnp.sum(part_hi, axis=0, keepdims=True)
    for c in range(3):
        tfar[c] = spread(20 + c)
        for a in range(4):
            tnear[a * 3 + c] = spread(8 + c * 4 + a)

    pl.semaphore_wait(barrier, 127 + 9)

    def send(src, dst, which, dev):
        pltpu.make_async_remote_copy(
            src_ref=src, dst_ref=dst, send_sem=ssem.at[which], recv_sem=rsem.at[which], device_id=dev, device_id_type=MESH
        ).start()

    def wait(ref, which):
        pltpu.make_async_copy(ref, ref, rsem.at[which]).wait()

    def drain(ref, which):
        pltpu.make_async_copy(ref, ref, ssem.at[which]).wait()

    def to_tiles(buf, which):
        for tt in tiles:
            send(buf.at[t], buf.at[t], which, (g, tt))

    def to_others(buf, which):
        for gg in others:
            send(buf.at[g], buf.at[g], which, (gg, t))

    def to_halo(buf, which):
        for tt in tiles:
            send(buf.at[4 + t], buf.at[8 + t], which, (left, tt))
            send(buf.at[4 + t], buf.at[t], which, (right, tt))
            send(buf.at[4 + t], buf.at[4 + t], which, (g, tt))
        send(buf.at[4 + t], buf.at[8 + t], which, (left, t))
        send(buf.at[4 + t], buf.at[t], which, (right, t))

    def neighbour(a, slot):
        rel = jnp.clip(lax.rem(near_ref[a, slot] - 4 * g + (4 + 512), 512), 0, 11)
        return rel // 4, lax.rem(rel, 4)

    def near_values():
        def body(i, carry):
            a, slot, tt = i // 16, lax.rem(i // 4, 4), lax.rem(i, 4)
            gg, leaf = neighbour(a, slot)
            src = hal1[gg * 4 + tt, leaf]
            d0 = tnear[a * 3] - src[0:1]
            d1 = tnear[a * 3 + 1] - src[1:2]
            d2 = tnear[a * 3 + 2] - src[2:3]
            gnear[i] = lax.rsqrt(d0 * d0 + d1 * d1 + d2 * d2 + spread_sq)
            return carry

        lax.fori_loop(0, 64, body, 0)

    def near_apply(value):
        def leaf_body(a, carry):
            def body(j, acc):
                slot, tt = j // 4, lax.rem(j, 4)
                gg, leaf = neighbour(a, slot)
                weight = jnp.where(slot < count_ref[a], near_scale, 0.0)
                return acc + gnear[a * 16 + j] * (value(gg * 4 + tt, leaf) * weight)

            acc_near[a] = lax.fori_loop(0, 16, body, jnp.zeros((128, 128), f32), unroll=4)
            return carry

        lax.fori_loop(0, 4, leaf_body, 0)

    def far_values():
        def body(b, carry):
            src = skb[b]
            d0 = tfar[0] - src[0:1]
            d1 = tfar[1] - src[1:2]
            d2 = tfar[2] - src[2:3]
            gfar[b] = lax.rsqrt(d0 * d0 + d1 * d1 + d2 * d2 + spread_sq)
            return carry

        lax.fori_loop(0, 128, body, 0)

    def far_apply(n):
        def body(b, acc):
            weight = jnp.where(mask_ref[0, b] != 0, far_scale, 0.0)
            return acc + gfar[b] * (cbuf[n, b] * weight)

        acc = lax.fori_loop(0, 128, body, jnp.zeros((128, 128), f32), unroll=8)
        return jnp.sum(acc.T, axis=0, keepdims=True)

    def coef_sum(n):
        mine = abuf[n, 0] + abuf[n, 1] + abuf[n, 2] + abuf[n, 3]
        cbuf[n, g] = jnp.where(own_half == 0, mine[0:1], mine[1:2])

    def finish(n):
        sky_lo = pbuf[n, 0] + pbuf[n, 1]
        sky_hi = pbuf[n, 2] + pbuf[n, 3]
        rows = jnp.zeros((128, 128), f32)
        part_lo = jnp.zeros((128, 128), f32)
        part_hi = jnp.zeros((128, 128), f32)
        for a in range(4):
            b_lo, b_hi = basis_ref[a, :, :128], basis_ref[a, :, 128:]
            total = acc_near[a] + b_lo * sky_lo + b_hi * sky_hi
            image = live_col[a] * (fcol[a] + jnp.sum(total, axis=1, keepdims=True))
            rows = jnp.where(lane == a, image, rows)
            if n == 0:
                fcol[a] = image
                part_lo = part_lo + b_lo * image
                part_hi = part_hi + b_hi * image
        if n == 0:
            abuf[1, t, 0:1] = jnp.sum(part_lo, axis=0, keepdims=True)
            abuf[1, t, 1:2] = jnp.sum(part_hi, axis=0, keepdims=True)
        return rows.T[0:4]

    to_tiles(abuf.at[0], COEF_ONE)
    to_halo(hal1, HALO_ONE)
    to_others(skb, SKEL)
    wait(abuf.at[0, pl.ds(0, 3)], COEF_ONE)
    coef_sum(0)
    to_others(cbuf.at[0], FAR_ONE)
    wait(skb.at[pl.ds(0, 127)], SKEL)
    far_values()
    wait(cbuf.at[0, pl.ds(0, 127)], FAR_ONE)
    pbuf[0, t] = far_apply(0)
    to_tiles(pbuf.at[0], SKY_ONE)
    wait(hal1.at[pl.ds(0, 11)], HALO_ONE)
    near_values()
    near_apply(lambda slot, leaf: hal1[slot, leaf][3:4])
    wait(pbuf.at[0, pl.ds(0, 3)], SKY_ONE)
    a_row = finish(0)

    to_tiles(abuf.at[1], COEF_TWO)
    for a in range(4):
        hal2[4 + t, a] = a_row[a : a + 1]
    to_halo(hal2, HALO_TWO)
    wait(abuf.at[1, pl.ds(0, 3)], COEF_TWO)
    coef_sum(1)
    to_others(cbuf.at[1], FAR_TWO)
    wait(hal2.at[pl.ds(0, 11)], HALO_TWO)
    near_apply(lambda slot, leaf: hal2[slot, leaf])
    wait(cbuf.at[1, pl.ds(0, 127)], FAR_TWO)
    pbuf[1, t] = far_apply(1)
    to_tiles(pbuf.at[1], SKY_TWO)
    wait(pbuf.at[1, pl.ds(0, 3)], SKY_TWO)
    b_row = finish(1)

    pairs = [s_row * s_row, s_row * a_row, s_row * b_row, a_row * a_row, a_row * b_row, b_row * b_row]
    sums = jnp.concatenate([jnp.sum(p, axis=0, keepdims=True) for p in pairs] + [jnp.zeros((2, 128), f32)], axis=0)
    sums = jnp.sum(sums, axis=1, keepdims=True)
    picked = lax.broadcasted_iota(jnp.int32, (8, 128), 0) == lax.broadcasted_iota(jnp.int32, (8, 128), 1)
    rtile[t] = jnp.sum(jnp.where(picked, sums, 0.0), axis=0, keepdims=True)
    to_tiles(rtile, SUM_TILE)
    wait(rtile.at[pl.ds(0, 3)], SUM_TILE)
    rblk[g] = rtile[0] + rtile[1] + rtile[2] + rtile[3]
    to_others(rblk, SUM_BLK)
    wait(rblk.at[pl.ds(0, 127)], SUM_BLK)
    dots = jnp.sum(rblk[...], axis=0)
    ss, sa, sb, aa, ab, bb = [dots[:, i : i + 1] for i in range(6)]

    beta_sq = ss + norm_eps
    beta = jnp.sqrt(beta_sq)
    h11 = sa / beta_sq
    h21_sq = jnp.maximum((aa - 2.0 * h11 * sa + h11 * h11 * ss) / beta_sq, 0.0) + norm_eps
    h21 = jnp.sqrt(h21_sq)
    h12 = (sb - h11 * sa) / (beta_sq * h21)
    h22 = (ab - h11 * aa - h11 * sb + h11 * h11 * sa) / (beta_sq * h21_sq)
    w_sq = (bb - 2.0 * h11 * ab + h11 * h11 * aa) / (beta_sq * h21_sq)
    first_sq = ss / beta_sq
    second_sq = (h21_sq - norm_eps) / h21_sq
    cross = h11 * (1.0 - first_sq) / h21
    rest_sq = w_sq - h12 * h12 * (2.0 - first_sq) - h22 * h22 * (2.0 - second_sq) + 2.0 * h12 * h22 * cross
    h32_sq = jnp.maximum(rest_sq, 0.0) + norm_eps
    m_aa = h11 * h11 + h21_sq
    m_ab = h11 * h12 + h21 * h22
    m_bb = h12 * h12 + h22 * h22 + h32_sq
    determ = m_aa * m_bb - m_ab * m_ab
    y_one = beta * (m_bb * h11 - m_ab * h12) / determ
    y_two = beta * (m_aa * h12 - m_ab * h11) / determ
    c_one = y_one / beta
    c_two = y_two / (beta * h21)
    sol_ref[...] = c_one * s_row + c_two * (a_row - h11 * s_row)
    res_ref[...] = s_row - c_one * a_row - c_two * (b_row - h11 * a_row)

    drain(hal1.at[pl.ds(0, 11)], HALO_ONE)
    drain(hal2.at[pl.ds(0, 11)], HALO_TWO)
    drain(abuf.at[0, pl.ds(0, 3)], COEF_ONE)
    drain(abuf.at[1, pl.ds(0, 3)], COEF_TWO)
    drain(skb.at[pl.ds(0, 127)], SKEL)
    drain(cbuf.at[0, pl.ds(0, 127)], FAR_ONE)
    drain(cbuf.at[1, pl.ds(0, 127)], FAR_TWO)
    drain(pbuf.at[0, pl.ds(0, 3)], SKY_ONE)
    drain(pbuf.at[1, pl.ds(0, 3)], SKY_TWO)
    drain(rtile.at[pl.ds(0, 3)], SUM_TILE)
    drain(rblk.at[pl.ds(0, 127)], SUM_BLK)


def per_device(right_side, points, basis, skeleton, cluster_sizes, near_list, near_count, far_mask):
    vmem = pl.BlockSpec(memory_space=pltpu.VMEM)
    smem = pl.BlockSpec(memory_space=pltpu.SMEM)
    out = jax.ShapeDtypeStruct((4, 128), f32)
    return pl.pallas_call(
        kernel,
        out_shape=(out, out),
        in_specs=[vmem] * 4 + [smem] * 4,
        out_specs=(vmem, vmem),
        scratch_shapes=[
            pltpu.VMEM((12, 4, 4, 128), f32),
            pltpu.VMEM((12, 4, 1, 128), f32),
            pltpu.VMEM((2, 4, 2, 128), f32),
            pltpu.VMEM((128, 4, 128), f32),
            pltpu.VMEM((2, 128, 1, 128), f32),
            pltpu.VMEM((2, 4, 1, 128), f32),
            pltpu.VMEM((4, 1, 128), f32),
            pltpu.VMEM((128, 1, 128), f32),
            pltpu.VMEM((128, 128, 128), f32),
            pltpu.VMEM((64, 128, 128), f32),
            pltpu.VMEM((3, 128, 128), f32),
            pltpu.VMEM((12, 128, 128), f32),
            pltpu.VMEM((4, 128, 128), f32),
            pltpu.VMEM((4, 128, 128), f32),
            pltpu.VMEM((4, 128, 128), f32),
            pltpu.SemaphoreType.DMA((EXCHANGES,)),
            pltpu.SemaphoreType.DMA((EXCHANGES,)),
        ],
        compiler_params=pltpu.CompilerParams(collective_id=0, has_side_effects=True, vmem_limit_bytes=48 * 2**20),
    )(right_side, points, basis, skeleton, cluster_sizes, near_list, near_count, far_mask)


def solution(mesh):
    placed = (
        P("blk", "tile"),
        P(None, "blk", "tile"),
        P("blk", "tile", None),
        P("blk", None, None),
        P("blk"),
        P("blk", None),
        P("blk"),
        P("blk", None),
    )
    return jax.shard_map(
        per_device,
        mesh=mesh,
        in_specs=placed,
        out_specs=(P("blk", "tile"), P("blk", "tile")),
        check_vma=False,
    )
```

```python
import functools
import math

import jax
import jax.numpy as jnp
from jax import lax
from jax.experimental import pallas as pl
from jax.experimental.pallas import tpu as pltpu
from jax.sharding import PartitionSpec as P

MESH = pl.DeviceIdType.MESH
f32 = jnp.float32
spread_sq = 0.25
norm_eps = 1e-06

HALO_ONE, HALO_TWO, COEF_ONE, COEF_TWO, SKEL, FAR_ONE, FAR_TWO, SKY_ONE, SKY_TWO, SUM_TILE, SUM_BLK = range(11)
EXCHANGES = 11


def hops(step):
    dx, dyl, dz, dc = step
    return min(dx, 4 - dx) + dyl + min(dz, 8 - dz)


OTHERS = sorted(
    [(dx, dyl, dz, dc) for dx in range(4) for dyl in range(2) for dz in range(8) for dc in range(2) if dx or dyl or dz or dc],
    key=lambda step: -hops(step),
)


def kernel(
    rs_hbm, pts_hbm, basis_hbm, skel_hbm, sizes_hbm, near_hbm, count_hbm, mask_hbm,
    out_ref,
    rs_ref, pts_ref, basis_ref, skel_ref, sizes_ref, near_ref, count_ref, mask_ref,
    hal1, hal2, abuf, skb, cbuf, pbuf, rtile, rblk,
    gfar, gnear, tfar, tnear, fcol, live_col, acc_near,
    ssem, rsem, lsem,
):
    g = lax.axis_index("blk")
    t = lax.axis_index("tile")
    near_scale = 2.0 / math.sqrt(512 * 4)
    far_scale = 4.0 / math.sqrt(256 * 128)

    loads = [
        pltpu.make_async_copy(src, dst, lsem.at[i])
        for i, (src, dst) in enumerate(
            [(sizes_hbm, sizes_ref), (rs_hbm, rs_ref), (basis_hbm, basis_ref), (pts_hbm, pts_ref), (skel_hbm, skel_ref),
             (near_hbm, near_ref), (count_hbm, count_ref), (mask_hbm, mask_ref)]
        )
    ]
    for load in loads:
        load.start()

    core, z, x, yl = lax.rem(g, 2), lax.rem(g // 2, 8), lax.rem(g // 16, 4), g // 64
    low = {(dz, dc): lax.rem(z + dz, 8) * 2 + lax.rem(core + dc, 2) for dz in range(8) for dc in range(2)}
    high = {(dx, dy): lax.rem(yl + dy, 2) * 64 + lax.rem(x + dx, 4) * 16 for dx in range(4) for dy in range(2)}
    others = [high[s[0], s[1]] + low[s[2], s[3]] for s in OTHERS]
    tiles = [lax.rem(t + d, 4) for d in (2, 1, 3)]
    left, right = lax.rem(g + 127, 128), lax.rem(g + 1, 128)

    barrier = pltpu.get_barrier_semaphore()
    for tt in tiles:
        for gg in (left, right, g):
            pl.semaphore_signal(barrier, inc=1, device_id=(gg, tt), device_id_type=MESH)
    for gg in others:
        pl.semaphore_signal(barrier, inc=1, device_id=(gg, t), device_id_type=MESH)

    loads[0].wait()
    loads[1].wait()
    col = lax.broadcasted_iota(jnp.int32, (1, 128), 1) + t * 128
    live_row = jnp.concatenate([(col < sizes_ref[a]).astype(f32) for a in range(4)], axis=0)
    s_row = live_row * rs_ref[...]
    own_half = lax.rem(t, 2)
    goal_half = t // 2
    lane = lax.broadcasted_iota(jnp.int32, (128, 128), 1)

    def columns(rows):
        return jnp.concatenate(rows + [jnp.zeros((128 - sum(r.shape[0] for r in rows), 128), f32)], axis=0).T

    def spread(cols, i):
        return jnp.broadcast_to(cols[:, i : i + 1], (128, 128))

    cols = columns([s_row, live_row])
    loads[2].wait()
    part_lo = jnp.zeros((128, 128), f32)
    part_hi = jnp.zeros((128, 128), f32)
    for a in range(4):
        s_b = spread(cols, a)
        fcol[a] = s_b
        live_col[a] = spread(cols, 4 + a)
        part_lo = part_lo + basis_ref[a, :, :128] * s_b
        part_hi = part_hi + basis_ref[a, :, 128:] * s_b
    abuf[0, t, 0:1] = jnp.sum(part_lo, axis=0, keepdims=True)
    abuf[0, t, 1:2] = jnp.sum(part_hi, axis=0, keepdims=True)
    for load in loads[3:]:
        load.wait()
    for a in range(4):
        hal1[4 + t, a] = jnp.concatenate([pts_ref[c, a : a + 1, :] for c in range(3)] + [s_row[a : a + 1]], axis=0)
    sk_lo = jnp.concatenate([skel_ref[c, :, :128] for c in range(3)], axis=0)
    sk_hi = jnp.concatenate([skel_ref[c, :, 128:] for c in range(3)], axis=0)
    goals = jnp.where(goal_half == 0, sk_lo, sk_hi)
    skb[g, 0:3] = jnp.where(own_half == 0, sk_lo, sk_hi)

    pl.semaphore_wait(barrier, 127 + 9)

    def send(src, dst, which, dev):
        pltpu.make_async_remote_copy(
            src_ref=src, dst_ref=dst, send_sem=ssem.at[which], recv_sem=rsem.at[which], device_id=dev, device_id_type=MESH
        ).start()

    def wait(ref, which):
        pltpu.make_async_copy(ref, ref, rsem.at[which]).wait()

    def drain(ref, which):
        pltpu.make_async_copy(ref, ref, ssem.at[which]).wait()

    def to_tiles(buf, which):
        for tt in tiles:
            send(buf.at[t], buf.at[t], which, (g, tt))

    def to_others(buf, which):
        for gg in others:
            send(buf.at[g], buf.at[g], which, (gg, t))

    def to_halo(buf, which):
        for tt in tiles:
            send(buf.at[4 + t], buf.at[8 + t], which, (left, tt))
            send(buf.at[4 + t], buf.at[t], which, (right, tt))
            send(buf.at[4 + t], buf.at[4 + t], which, (g, tt))
        send(buf.at[4 + t], buf.at[8 + t], which, (left, t))
        send(buf.at[4 + t], buf.at[t], which, (right, t))

    def neighbour(a, slot):
        rel = jnp.clip(lax.rem(near_ref[a, slot] - 4 * g + (4 + 512), 512), 0, 11)
        return rel // 4, lax.rem(rel, 4)

    def near_values():
        def body(i, carry):
            a, slot, tt = i // 16, lax.rem(i // 4, 4), lax.rem(i, 4)
            gg, leaf = neighbour(a, slot)
            src = hal1[gg * 4 + tt, leaf]
            d0 = tnear[a * 3] - src[0:1]
            d1 = tnear[a * 3 + 1] - src[1:2]
            d2 = tnear[a * 3 + 2] - src[2:3]
            gnear[i] = lax.rsqrt(d0 * d0 + d1 * d1 + d2 * d2 + spread_sq)
            return carry

        lax.fori_loop(0, 64, body, 0)

    def near_apply(value):
        def leaf_body(a, carry):
            def body(j, acc):
                slot, tt = j // 4, lax.rem(j, 4)
                gg, leaf = neighbour(a, slot)
                weight = jnp.where(slot < count_ref[a], near_scale, 0.0)
                return acc + gnear[a * 16 + j] * (value(gg * 4 + tt, leaf) * weight)

            acc_near[a] = lax.fori_loop(0, 16, body, jnp.zeros((128, 128), f32), unroll=4)
            return carry

        lax.fori_loop(0, 4, leaf_body, 0)

    def far_values():
        def body(b, carry):
            src = skb[b]
            d0 = tfar[0] - src[0:1]
            d1 = tfar[1] - src[1:2]
            d2 = tfar[2] - src[2:3]
            gfar[b] = lax.rsqrt(d0 * d0 + d1 * d1 + d2 * d2 + spread_sq)
            return carry

        lax.fori_loop(0, 128, body, 0)

    def far_apply(n):
        def body(b, acc):
            weight = jnp.where(mask_ref[0, b] != 0, far_scale, 0.0)
            return acc + gfar[b] * (cbuf[n, b] * weight)

        acc = lax.fori_loop(0, 128, body, jnp.zeros((128, 128), f32), unroll=8)
        return jnp.sum(acc.T, axis=0, keepdims=True)

    def coef_sum(n):
        mine = abuf[n, 0] + abuf[n, 1] + abuf[n, 2] + abuf[n, 3]
        cbuf[n, g] = jnp.where(own_half == 0, mine[0:1], mine[1:2])

    def finish(n):
        sky_lo = pbuf[n, 0] + pbuf[n, 1]
        sky_hi = pbuf[n, 2] + pbuf[n, 3]
        rows = jnp.zeros((128, 128), f32)
        part_lo = jnp.zeros((128, 128), f32)
        part_hi = jnp.zeros((128, 128), f32)
        for a in range(4):
            b_lo, b_hi = basis_ref[a, :, :128], basis_ref[a, :, 128:]
            total = acc_near[a] + b_lo * sky_lo + b_hi * sky_hi
            image = live_col[a] * (fcol[a] + jnp.sum(total, axis=1, keepdims=True))
            rows = jnp.where(lane == a, image, rows)
            if n == 0:
                fcol[a] = image
                part_lo = part_lo + b_lo * image
                part_hi = part_hi + b_hi * image
        if n == 0:
            abuf[1, t, 0:1] = jnp.sum(part_lo, axis=0, keepdims=True)
            abuf[1, t, 1:2] = jnp.sum(part_hi, axis=0, keepdims=True)
        return rows.T[0:4]

    to_tiles(abuf.at[0], COEF_ONE)
    to_halo(hal1, HALO_ONE)
    for gg in others:
        send(skb.at[g, pl.ds(0, 3)], skb.at[g, pl.ds(0, 3)], SKEL, (gg, t))
    cols = columns([pts_ref[c] for c in range(3)] + [goals])
    for c in range(3):
        tfar[c] = spread(cols, 12 + c)
        for a in range(4):
            tnear[a * 3 + c] = spread(cols, c * 4 + a)
    wait(abuf.at[0, pl.ds(0, 3)], COEF_ONE)
    coef_sum(0)
    to_others(cbuf.at[0], FAR_ONE)
    wait(skb.at[pl.ds(0, 127), pl.ds(0, 3)], SKEL)
    far_values()
    wait(cbuf.at[0, pl.ds(0, 127)], FAR_ONE)
    pbuf[0, t] = far_apply(0)
    to_tiles(pbuf.at[0], SKY_ONE)
    wait(hal1.at[pl.ds(0, 11)], HALO_ONE)
    near_values()
    near_apply(lambda slot, leaf: hal1[slot, leaf][3:4])
    wait(pbuf.at[0, pl.ds(0, 3)], SKY_ONE)
    a_row = finish(0)

    to_tiles(abuf.at[1], COEF_TWO)
    for a in range(4):
        hal2[4 + t, a] = a_row[a : a + 1]
    to_halo(hal2, HALO_TWO)
    wait(abuf.at[1, pl.ds(0, 3)], COEF_TWO)
    coef_sum(1)
    to_others(cbuf.at[1], FAR_TWO)
    wait(hal2.at[pl.ds(0, 11)], HALO_TWO)
    near_apply(lambda slot, leaf: hal2[slot, leaf])
    wait(cbuf.at[1, pl.ds(0, 127)], FAR_TWO)
    pbuf[1, t] = far_apply(1)
    to_tiles(pbuf.at[1], SKY_TWO)
    wait(pbuf.at[1, pl.ds(0, 3)], SKY_TWO)
    b_row = finish(1)

    pairs = [s_row * s_row, s_row * a_row, s_row * b_row, a_row * a_row, a_row * b_row, b_row * b_row]
    sums = jnp.concatenate([jnp.sum(p, axis=0, keepdims=True) for p in pairs] + [jnp.zeros((2, 128), f32)], axis=0)
    sums = jnp.sum(sums, axis=1, keepdims=True)
    picked = lax.broadcasted_iota(jnp.int32, (8, 128), 0) == lax.broadcasted_iota(jnp.int32, (8, 128), 1)
    rtile[t] = jnp.sum(jnp.where(picked, sums, 0.0), axis=0, keepdims=True)
    to_tiles(rtile, SUM_TILE)
    wait(rtile.at[pl.ds(0, 3)], SUM_TILE)
    rblk[g] = rtile[0] + rtile[1] + rtile[2] + rtile[3]
    to_others(rblk, SUM_BLK)
    wait(rblk.at[pl.ds(0, 127)], SUM_BLK)
    dots = jnp.sum(rblk[...], axis=0)
    ss, sa, sb, aa, ab, bb = [dots[:, i : i + 1] for i in range(6)]

    beta_sq = ss + norm_eps
    beta = jnp.sqrt(beta_sq)
    h11 = sa / beta_sq
    h21_sq = jnp.maximum((aa - 2.0 * h11 * sa + h11 * h11 * ss) / beta_sq, 0.0) + norm_eps
    h21 = jnp.sqrt(h21_sq)
    h12 = (sb - h11 * sa) / (beta_sq * h21)
    h22 = (ab - h11 * aa - h11 * sb + h11 * h11 * sa) / (beta_sq * h21_sq)
    w_sq = (bb - 2.0 * h11 * ab + h11 * h11 * aa) / (beta_sq * h21_sq)
    first_sq = ss / beta_sq
    second_sq = (h21_sq - norm_eps) / h21_sq
    cross = h11 * (1.0 - first_sq) / h21
    rest_sq = w_sq - h12 * h12 * (2.0 - first_sq) - h22 * h22 * (2.0 - second_sq) + 2.0 * h12 * h22 * cross
    h32_sq = jnp.maximum(rest_sq, 0.0) + norm_eps
    m_aa = h11 * h11 + h21_sq
    m_ab = h11 * h12 + h21 * h22
    m_bb = h12 * h12 + h22 * h22 + h32_sq
    determ = m_aa * m_bb - m_ab * m_ab
    y_one = beta * (m_bb * h11 - m_ab * h12) / determ
    y_two = beta * (m_aa * h12 - m_ab * h11) / determ
    c_one = y_one / beta
    c_two = y_two / (beta * h21)
    out_ref[0:4] = c_one * s_row + c_two * (a_row - h11 * s_row)
    out_ref[4:8] = s_row - c_one * a_row - c_two * (b_row - h11 * a_row)

    drain(hal1.at[pl.ds(0, 11)], HALO_ONE)
    drain(hal2.at[pl.ds(0, 11)], HALO_TWO)
    drain(abuf.at[0, pl.ds(0, 3)], COEF_ONE)
    drain(abuf.at[1, pl.ds(0, 3)], COEF_TWO)
    drain(skb.at[pl.ds(0, 127), pl.ds(0, 3)], SKEL)
    drain(cbuf.at[0, pl.ds(0, 127)], FAR_ONE)
    drain(cbuf.at[1, pl.ds(0, 127)], FAR_TWO)
    drain(pbuf.at[0, pl.ds(0, 3)], SKY_ONE)
    drain(pbuf.at[1, pl.ds(0, 3)], SKY_TWO)
    drain(rtile.at[pl.ds(0, 3)], SUM_TILE)
    drain(rblk.at[pl.ds(0, 127)], SUM_BLK)


def per_device(right_side, points, basis, skeleton, cluster_sizes, near_list, near_count, far_mask):
    vmem = pl.BlockSpec(memory_space=pltpu.VMEM)
    hbm = pl.BlockSpec(memory_space=pltpu.HBM)
    both = pl.pallas_call(
        kernel,
        out_shape=jax.ShapeDtypeStruct((8, 128), f32),
        in_specs=[hbm] * 8,
        out_specs=vmem,
        scratch_shapes=[
            pltpu.VMEM((4, 128), f32),
            pltpu.VMEM((3, 4, 128), f32),
            pltpu.VMEM((4, 128, 256), f32),
            pltpu.VMEM((3, 1, 256), f32),
            pltpu.SMEM((4,), jnp.int32),
            pltpu.SMEM((4, 4), jnp.int32),
            pltpu.SMEM((4,), jnp.int32),
            pltpu.SMEM((1, 128), jnp.int32),
            pltpu.VMEM((12, 4, 4, 128), f32),
            pltpu.VMEM((12, 4, 1, 128), f32),
            pltpu.VMEM((2, 4, 2, 128), f32),
            pltpu.VMEM((128, 4, 128), f32),
            pltpu.VMEM((2, 128, 1, 128), f32),
            pltpu.VMEM((2, 4, 1, 128), f32),
            pltpu.VMEM((4, 1, 128), f32),
            pltpu.VMEM((128, 1, 128), f32),
            pltpu.VMEM((128, 128, 128), f32),
            pltpu.VMEM((64, 128, 128), f32),
            pltpu.VMEM((3, 128, 128), f32),
            pltpu.VMEM((12, 128, 128), f32),
            pltpu.VMEM((4, 128, 128), f32),
            pltpu.VMEM((4, 128, 128), f32),
            pltpu.VMEM((4, 128, 128), f32),
            pltpu.SemaphoreType.DMA((EXCHANGES,)),
            pltpu.SemaphoreType.DMA((EXCHANGES,)),
            pltpu.SemaphoreType.DMA((8,)),
        ],
        compiler_params=pltpu.CompilerParams(collective_id=0, has_side_effects=True, vmem_limit_bytes=64 * 2**20),
    )(right_side, points, basis, skeleton.transpose(1, 0, 2), cluster_sizes, near_list, near_count, far_mask)
    return both[0:4], both[4:8]


def solution(mesh):
    placed = (
        P("blk", "tile"),
        P(None, "blk", "tile"),
        P("blk", "tile", None),
        P("blk", None, None),
        P("blk"),
        P("blk", None),
        P("blk"),
        P("blk", None),
    )
    return jax.shard_map(
        per_device,
        mesh=mesh,
        in_specs=placed,
        out_specs=(P("blk", "tile"), P("blk", "tile")),
        check_vma=False,
    )
```

```python
import functools
import math

import jax
import jax.numpy as jnp
from jax import lax
from jax.experimental import pallas as pl
from jax.experimental.pallas import tpu as pltpu
from jax.sharding import PartitionSpec as P

MESH = pl.DeviceIdType.MESH
f32 = jnp.float32
spread_sq = 0.25
norm_eps = 1e-06

HALO_ONE, HALO_TWO, COEF, SKEL, FAR_ONE, FAR_TWO, SKY_ONE, SKY_TWO, MIX_PART, MIX_ALL, SUMS = range(11)
EXCHANGES = 11


def hops(step):
    dx, dyl, dz, dc = step
    return min(dx, 4 - dx) + dyl + min(dz, 8 - dz)


OTHERS = sorted(
    [(dx, dyl, dz, dc) for dx in range(4) for dyl in range(2) for dz in range(8) for dc in range(2) if dx or dyl or dz or dc],
    key=lambda step: -hops(step),
)


def kernel(
    rs_hbm, pts_hbm, basis_hbm, skel_hbm, sizes_hbm, near_hbm, count_hbm, mask_hbm,
    out_ref,
    rs_ref, pts_ref, basis_ref, skel_ref, sizes_ref, near_ref, count_ref, mask_ref,
    hal1, hal2, abuf, skb, cbuf, pbuf, rblk, mix_own, mix_part, mix_all, mix,
    gfar, gnear, tfar, tnear, scol, ucol, acol, live_col,
    ssem, rsem, lsem,
):
    g = lax.axis_index("blk")
    t = lax.axis_index("tile")
    near_scale = 2.0 / math.sqrt(512 * 4)
    far_scale = 4.0 / math.sqrt(256 * 128)

    loads = [
        pltpu.make_async_copy(src, dst, lsem.at[i])
        for i, (src, dst) in enumerate(
            [(sizes_hbm, sizes_ref), (rs_hbm, rs_ref), (basis_hbm, basis_ref), (pts_hbm, pts_ref), (skel_hbm, skel_ref),
             (near_hbm, near_ref), (count_hbm, count_ref), (mask_hbm, mask_ref)]
        )
    ]
    for load in loads:
        load.start()

    core, z, x, yl = lax.rem(g, 2), lax.rem(g // 2, 8), lax.rem(g // 16, 4), g // 64
    low = {(dz, dc): lax.rem(z + dz, 8) * 2 + lax.rem(core + dc, 2) for dz in range(8) for dc in range(2)}
    high = {(dx, dy): lax.rem(yl + dy, 2) * 64 + lax.rem(x + dx, 4) * 16 for dx in range(4) for dy in range(2)}
    others = [high[s[0], s[1]] + low[s[2], s[3]] for s in OTHERS]
    tiles = [lax.rem(t + d, 4) for d in (2, 1, 3)]
    left, right = lax.rem(g + 127, 128), lax.rem(g + 1, 128)

    barrier = pltpu.get_barrier_semaphore()
    for tt in tiles:
        for gg in (left, right, g):
            pl.semaphore_signal(barrier, inc=1, device_id=(gg, tt), device_id_type=MESH)
    for gg in others:
        pl.semaphore_signal(barrier, inc=1, device_id=(gg, t), device_id_type=MESH)

    loads[0].wait()
    loads[1].wait()
    col = lax.broadcasted_iota(jnp.int32, (1, 128), 1) + t * 128
    live_row = jnp.concatenate([(col < sizes_ref[a]).astype(f32) for a in range(4)], axis=0)
    s_row = live_row * rs_ref[...]
    own_half = lax.rem(t, 2)
    goal_half = t // 2
    lane = lax.broadcasted_iota(jnp.int32, (128, 128), 1)

    def columns(rows):
        return jnp.concatenate(rows + [jnp.zeros((128 - sum(r.shape[0] for r in rows), 128), f32)], axis=0).T

    def spread(cols, i):
        return jnp.broadcast_to(cols[:, i : i + 1], (128, 128))

    cols = columns([s_row, live_row])
    loads[2].wait()
    part_lo = jnp.zeros((128, 128), f32)
    part_hi = jnp.zeros((128, 128), f32)
    s_sq = jnp.zeros((128, 128), f32)
    for a in range(4):
        s_b = spread(cols, a)
        scol[a] = s_b
        s_sq = s_sq + s_b * s_b
        live_col[a] = spread(cols, 4 + a)
        part_lo = part_lo + basis_ref[a, :, :128] * s_b
        part_hi = part_hi + basis_ref[a, :, 128:] * s_b
    abuf[t, 0:1] = jnp.sum(part_lo, axis=0, keepdims=True)
    abuf[t, 1:2] = jnp.sum(part_hi, axis=0, keepdims=True)
    abuf[t, 2:3] = jnp.sum(s_sq, axis=0, keepdims=True)
    abuf[t, 3:4] = jnp.zeros((1, 128), f32)
    for load in loads[3:]:
        load.wait()
    for a in range(4):
        hal1[4 + t, a] = jnp.concatenate([pts_ref[c, a : a + 1, :] for c in range(3)] + [s_row[a : a + 1]], axis=0)
    sk_lo = jnp.concatenate([skel_ref[c, :, :128] for c in range(3)], axis=0)
    sk_hi = jnp.concatenate([skel_ref[c, :, 128:] for c in range(3)], axis=0)
    goals = jnp.where(goal_half == 0, sk_lo, sk_hi)
    skb[g, 0:3] = jnp.where(own_half == 0, sk_lo, sk_hi)

    pl.semaphore_wait(barrier, 127 + 9)

    def send(src, dst, which, dev):
        pltpu.make_async_remote_copy(
            src_ref=src, dst_ref=dst, send_sem=ssem.at[which], recv_sem=rsem.at[which], device_id=dev, device_id_type=MESH
        ).start()

    def wait(ref, which):
        pltpu.make_async_copy(ref, ref, rsem.at[which]).wait()

    def drain(ref, which):
        pltpu.make_async_copy(ref, ref, ssem.at[which]).wait()

    def to_tiles(buf, which):
        for tt in tiles:
            send(buf.at[t], buf.at[t], which, (g, tt))

    def to_others(buf, which):
        for gg in others:
            send(buf.at[g], buf.at[g], which, (gg, t))

    def to_halo(buf, which):
        for tt in tiles:
            send(buf.at[4 + t], buf.at[8 + t], which, (left, tt))
            send(buf.at[4 + t], buf.at[t], which, (right, tt))
            send(buf.at[4 + t], buf.at[4 + t], which, (g, tt))
        send(buf.at[4 + t], buf.at[8 + t], which, (left, t))
        send(buf.at[4 + t], buf.at[t], which, (right, t))

    def neighbour(a, slot):
        rel = jnp.clip(lax.rem(near_ref[a, slot] - 4 * g + (4 + 512), 512), 0, 11)
        return rel // 4, lax.rem(rel, 4)

    def kernel_values(base, first, src):
        x, y, z = src[0:1], src[1:2], src[2:3]
        size = x * x + y * y + z * z + spread_sq
        return lax.rsqrt((base[first] + size) + (base[first + 1] * x + base[first + 2] * y + base[first + 3] * z))

    def near_apply(field, visit):
        for a in range(4):
            def body(slot, acc, a=a):
                gg, leaf = neighbour(a, slot)
                weight = jnp.where(slot < count_ref[a], near_scale, 0.0)
                for tt in range(4):
                    values, source = visit(a, slot, tt, gg * 4 + tt, leaf)
                    acc = acc + values * (source * weight)
                return acc

            acc = lax.fori_loop(0, 4, body, jnp.zeros((128, 128), f32), unroll=2)
            ucol[a] = live_col[a] * (field[a] + jnp.sum(acc, axis=1, keepdims=True))

    def near_first():
        def visit(a, slot, tt, place, leaf):
            src = hal1[place, leaf]
            values = kernel_values(tnear, a * 4, src)
            gnear[a * 16 + slot * 4 + tt] = values
            return values, src[3:4]

        near_apply(scol, visit)

    def near_second():
        near_apply(acol, lambda a, slot, tt, place, leaf: (gnear[a * 16 + slot * 4 + tt], hal2[place, leaf]))

    def far_values():
        def body(b, carry):
            gfar[b] = kernel_values(tfar, 0, skb[b])
            return carry

        lax.fori_loop(0, 128, body, 0, unroll=4)

    def far_apply(n):
        def body(b, acc):
            weight = jnp.where(mask_ref[0, b] != 0, far_scale, 0.0)
            return acc + gfar[b] * (cbuf[n, b] * weight)

        acc = lax.fori_loop(0, 128, body, jnp.zeros((128, 128), f32), unroll=8)
        return jnp.sum(acc.T, axis=0, keepdims=True)

    def near_parts(n, fields):
        lo = jnp.zeros((128, 128), f32)
        hi = jnp.zeros((128, 128), f32)
        prods = [jnp.zeros((128, 128), f32) for _ in range(len(fields) + 1)]
        for a in range(4):
            u = ucol[a]
            lo = lo + basis_ref[a, :, :128] * u
            hi = hi + basis_ref[a, :, 128:] * u
            for i, field in enumerate(fields + [ucol]):
                prods[i] = prods[i] + field[a] * u
        pbuf[n, t, 1:2] = jnp.sum(lo, axis=0, keepdims=True)
        pbuf[n, t, 2:3] = jnp.sum(hi, axis=0, keepdims=True)
        packed = jnp.zeros((1, 128), f32)
        for i, prod in enumerate(prods):
            packed = jnp.where(lane[0:1] == i, jnp.sum(prod, axis=0, keepdims=True), packed)
        pbuf[n, t, 3:4] = packed

    def gathered(n):
        low, high = pbuf[n, 0] + pbuf[n, 1], pbuf[n, 2] + pbuf[n, 3]
        both = low + high
        return low[0:1], high[0:1], both[1:2], both[2:3], both[3:4]

    def mixed(sky_lo, sky_hi):
        pair = columns([sky_lo, sky_hi])
        col_lo, col_hi = spread(pair, 0), spread(pair, 1)
        lo = mix[0] * col_lo + mix[1] * col_hi
        hi = mix[2] * col_lo + mix[3] * col_hi
        return jnp.sum(lo, axis=0, keepdims=True), jnp.sum(hi, axis=0, keepdims=True)

    def image(sky_lo, sky_hi, keep):
        rows = jnp.zeros((128, 128), f32)
        for a in range(4):
            far = basis_ref[a, :, :128] * sky_lo + basis_ref[a, :, 128:] * sky_hi
            value = ucol[a] + live_col[a] * jnp.sum(far, axis=1, keepdims=True)
            rows = jnp.where(lane == a, value, rows)
            if keep:
                acol[a] = value
        return rows.T[0:4]

    to_tiles(abuf, COEF)
    to_halo(hal1, HALO_ONE)

    points_of = basis_ref[...].reshape(512, 256)
    masked = points_of * live_col[...].reshape(512, 128)[:, 0:1]

    def product(left, right):
        return lax.dot_general(
            left, right, (((0,), (0,)), ((), ())), precision=lax.Precision.HIGHEST, preferred_element_type=f32
        )

    upper = product(masked[:, :128], points_of)
    lower = product(masked[:, 128:], points_of[:, 128:])
    mix_own[0] = upper[0:96, :128]
    mix_own[1, 0:32] = upper[96:128, :128]
    mix_own[1, 32:96] = upper[0:64, 128:]
    mix_own[2, 0:64] = upper[64:128, 128:]
    mix_own[2, 64:96] = lower[0:32]
    mix_own[3] = lower[32:128]
    for tt in tiles:
        send(mix_own.at[tt], mix_part.at[t], MIX_PART, (g, tt))
    mix_part[t] = mix_own[t]
    for gg in others:
        send(skb.at[g, pl.ds(0, 3)], skb.at[g, pl.ds(0, 3)], SKEL, (gg, t))
    goal_rows = [goals[c : c + 1] for c in range(3)]
    cols = columns(
        [-2.0 * pts_ref[c] for c in range(3)] + [sum(pts_ref[c] * pts_ref[c] for c in range(3))]
        + [-2.0 * row for row in goal_rows] + [sum(row * row for row in goal_rows)]
    )
    for c in range(4):
        tfar[(c + 1) % 4] = spread(cols, 16 + c)
        for a in range(4):
            tnear[a * 4 + (c + 1) % 4] = spread(cols, c * 4 + a)

    wait(abuf.at[pl.ds(0, 3)], COEF)
    parts = abuf[0] + abuf[1] + abuf[2] + abuf[3]
    one_lo, one_hi, ss = parts[0:1], parts[1:2], parts[2:3]
    cbuf[0, g] = jnp.where(own_half == 0, one_lo, one_hi)
    to_others(cbuf.at[0], FAR_ONE)
    wait(hal1.at[pl.ds(0, 11)], HALO_ONE)
    near_first()
    wait(mix_part.at[pl.ds(0, 3)], MIX_PART)
    mix_all[t] = mix_part[0] + mix_part[1] + mix_part[2] + mix_part[3]
    to_tiles(mix_all, MIX_ALL)
    near_parts(0, [scol])
    wait(skb.at[pl.ds(0, 127), pl.ds(0, 3)], SKEL)
    far_values()
    wait(cbuf.at[0, pl.ds(0, 127)], FAR_ONE)
    pbuf[0, t, 0:1] = far_apply(0)
    to_tiles(pbuf.at[0], SKY_ONE)
    wait(mix_all.at[pl.ds(0, 3)], MIX_ALL)
    cross = jnp.concatenate([mix_all[1, 32:96], mix_all[2, 0:64]], axis=0)
    mix[0] = jnp.concatenate([mix_all[0], mix_all[1, 0:32]], axis=0)
    mix[1] = cross.T
    mix[2] = cross
    mix[3] = jnp.concatenate([mix_all[2, 64:96], mix_all[3]], axis=0)
    wait(pbuf.at[0, pl.ds(0, 3)], SKY_ONE)
    sky1_lo, sky1_hi, r1_lo, r1_hi, dots1 = gathered(0)
    a_row = image(sky1_lo, sky1_hi, True)

    for a in range(4):
        hal2[4 + t, a] = a_row[a : a + 1]
    to_halo(hal2, HALO_TWO)
    m1_lo, m1_hi = mixed(sky1_lo, sky1_hi)
    two_lo, two_hi = r1_lo + m1_lo, r1_hi + m1_hi
    cbuf[1, g] = jnp.where(own_half == 0, two_lo, two_hi)
    to_others(cbuf.at[1], FAR_TWO)
    wait(hal2.at[pl.ds(0, 11)], HALO_TWO)
    near_second()
    near_parts(1, [scol, acol])
    wait(cbuf.at[1, pl.ds(0, 127)], FAR_TWO)
    pbuf[1, t, 0:1] = far_apply(1)
    to_tiles(pbuf.at[1], SKY_TWO)
    wait(pbuf.at[1, pl.ds(0, 3)], SKY_TWO)
    sky2_lo, sky2_hi, r2_lo, r2_hi, dots2 = gathered(1)

    m2_lo, m2_hi = mixed(sky2_lo, sky2_hi)
    rows = [
        one_lo * sky1_lo + one_hi * sky1_hi,
        one_lo * sky2_lo + one_hi * sky2_hi,
        (r1_lo + two_lo) * sky1_lo + (r1_hi + two_hi) * sky1_hi,
        two_lo * sky2_lo + two_hi * sky2_hi,
        (2.0 * r2_lo + m2_lo) * sky2_lo + (2.0 * r2_hi + m2_hi) * sky2_hi,
    ]
    near_part = [dots1[:, 0:1], dots2[:, 0:1], dots1[:, 1:2], dots2[:, 1:2], dots2[:, 2:3]]
    far_part = jnp.sum(jnp.concatenate(rows + [jnp.zeros((3, 128), f32)], axis=0), axis=1, keepdims=True)
    packed = ss
    for i in range(5):
        packed = jnp.where(lane[0:1] == i + 1, near_part[i] + far_part[i : i + 1], packed)
    rblk[g] = packed
    to_others(rblk, SUMS)
    b_row = image(sky2_lo, sky2_hi, False)
    wait(rblk.at[pl.ds(0, 127)], SUMS)
    dots = jnp.sum(rblk[...], axis=0)
    ss, sa, sb, aa, ab, bb = [dots[:, i : i + 1] for i in range(6)]

    beta_sq = ss + norm_eps
    beta = jnp.sqrt(beta_sq)
    h11 = sa / beta_sq
    h21_sq = jnp.maximum((aa - 2.0 * h11 * sa + h11 * h11 * ss) / beta_sq, 0.0) + norm_eps
    h21 = jnp.sqrt(h21_sq)
    h12 = (sb - h11 * sa) / (beta_sq * h21)
    h22 = (ab - h11 * aa - h11 * sb + h11 * h11 * sa) / (beta_sq * h21_sq)
    w_sq = (bb - 2.0 * h11 * ab + h11 * h11 * aa) / (beta_sq * h21_sq)
    first_sq = ss / beta_sq
    second_sq = (h21_sq - norm_eps) / h21_sq
    cross_sq = h11 * (1.0 - first_sq) / h21
    rest_sq = w_sq - h12 * h12 * (2.0 - first_sq) - h22 * h22 * (2.0 - second_sq) + 2.0 * h12 * h22 * cross_sq
    h32_sq = jnp.maximum(rest_sq, 0.0) + norm_eps
    m_aa = h11 * h11 + h21_sq
    m_ab = h11 * h12 + h21 * h22
    m_bb = h12 * h12 + h22 * h22 + h32_sq
    determ = m_aa * m_bb - m_ab * m_ab
    y_one = beta * (m_bb * h11 - m_ab * h12) / determ
    y_two = beta * (m_aa * h12 - m_ab * h11) / determ
    c_one = y_one / beta
    c_two = y_two / (beta * h21)
    out_ref[0:4] = c_one * s_row + c_two * (a_row - h11 * s_row)
    out_ref[4:8] = s_row - c_one * a_row - c_two * (b_row - h11 * a_row)

    drain(hal1.at[pl.ds(0, 11)], HALO_ONE)
    drain(hal2.at[pl.ds(0, 11)], HALO_TWO)
    drain(abuf.at[pl.ds(0, 3)], COEF)
    drain(mix_part.at[pl.ds(0, 3)], MIX_PART)
    drain(mix_all.at[pl.ds(0, 3)], MIX_ALL)
    drain(skb.at[pl.ds(0, 127), pl.ds(0, 3)], SKEL)
    drain(cbuf.at[0, pl.ds(0, 127)], FAR_ONE)
    drain(cbuf.at[1, pl.ds(0, 127)], FAR_TWO)
    drain(pbuf.at[0, pl.ds(0, 3)], SKY_ONE)
    drain(pbuf.at[1, pl.ds(0, 3)], SKY_TWO)
    drain(rblk.at[pl.ds(0, 127)], SUMS)


def per_device(right_side, points, basis, skeleton, cluster_sizes, near_list, near_count, far_mask):
    vmem = pl.BlockSpec(memory_space=pltpu.VMEM)
    hbm = pl.BlockSpec(memory_space=pltpu.HBM)
    both = pl.pallas_call(
        kernel,
        out_shape=jax.ShapeDtypeStruct((8, 128), f32),
        in_specs=[hbm] * 8,
        out_specs=vmem,
        scratch_shapes=[
            pltpu.VMEM((4, 128), f32),
            pltpu.VMEM((3, 4, 128), f32),
            pltpu.VMEM((4, 128, 256), f32),
            pltpu.VMEM((3, 1, 256), f32),
            pltpu.SMEM((4,), jnp.int32),
            pltpu.SMEM((4, 4), jnp.int32),
            pltpu.SMEM((4,), jnp.int32),
            pltpu.SMEM((1, 128), jnp.int32),
            pltpu.VMEM((12, 4, 4, 128), f32),
            pltpu.VMEM((12, 4, 1, 128), f32),
            pltpu.VMEM((4, 4, 128), f32),
            pltpu.VMEM((128, 4, 128), f32),
            pltpu.VMEM((2, 128, 1, 128), f32),
            pltpu.VMEM((2, 4, 4, 128), f32),
            pltpu.VMEM((128, 1, 128), f32),
            pltpu.VMEM((4, 96, 128), f32),
            pltpu.VMEM((4, 96, 128), f32),
            pltpu.VMEM((4, 96, 128), f32),
            pltpu.VMEM((4, 128, 128), f32),
            pltpu.VMEM((128, 128, 128), f32),
            pltpu.VMEM((64, 128, 128), f32),
            pltpu.VMEM((4, 128, 128), f32),
            pltpu.VMEM((16, 128, 128), f32),
            pltpu.VMEM((4, 128, 128), f32),
            pltpu.VMEM((4, 128, 128), f32),
            pltpu.VMEM((4, 128, 128), f32),
            pltpu.VMEM((4, 128, 128), f32),
            pltpu.SemaphoreType.DMA((EXCHANGES,)),
            pltpu.SemaphoreType.DMA((EXCHANGES,)),
            pltpu.SemaphoreType.DMA((8,)),
        ],
        compiler_params=pltpu.CompilerParams(collective_id=0, has_side_effects=True, vmem_limit_bytes=64 * 2**20),
    )(right_side, points, basis, skeleton.transpose(1, 0, 2), cluster_sizes, near_list, near_count, far_mask)
    return both[0:4], both[4:8]


def solution(mesh):
    placed = (
        P("blk", "tile"),
        P(None, "blk", "tile"),
        P("blk", "tile", None),
        P("blk", None, None),
        P("blk"),
        P("blk", None),
        P("blk"),
        P("blk", None),
    )
    return jax.shard_map(
        per_device,
        mesh=mesh,
        in_specs=placed,
        out_specs=(P("blk", "tile"), P("blk", "tile")),
        check_vma=False,
    )
```

```python
import functools
import math

import jax
import jax.numpy as jnp
from jax import lax
from jax.experimental import pallas as pl
from jax.experimental.pallas import tpu as pltpu
from jax.sharding import PartitionSpec as P

MESH = pl.DeviceIdType.MESH
f32 = jnp.float32
spread_sq = 0.25
norm_eps = 1e-06

HALO_ONE, HALO_TWO, COEF, SKEL, SKEL_PAIR, FAR_ONE, FAR_TWO, SKY_ONE, SKY_TWO, MIX_PART, MIX_ALL, SUMS = range(12)
EXCHANGES = 12


def hops(step):
    dx, dyl, dz, dc = step
    return min(dx, 4 - dx) + dyl + min(dz, 8 - dz)


OTHERS = sorted(
    [(dx, dyl, dz, dc) for dx in range(4) for dyl in range(2) for dz in range(8) for dc in range(2) if dx or dyl or dz or dc],
    key=lambda step: -hops(step),
)


def kernel(
    rs_hbm, pts_hbm, basis_hbm, skel_hbm, sizes_hbm, near_hbm, count_hbm, mask_hbm,
    out_ref,
    rs_ref, pts_ref, basis_ref, skel_ref, sizes_ref, near_ref, count_ref, mask_ref,
    hal1, hal2, abuf, skb, cbuf, pbuf, rblk, mix_own, mix_part, mix_all, mix,
    gfar, gnear, tfar, tnear, scol, ucol, acol, live_col,
    ssem, rsem, lsem,
):
    g = lax.axis_index("blk")
    t = lax.axis_index("tile")
    near_scale = 2.0 / math.sqrt(512 * 4)
    far_scale = 4.0 / math.sqrt(256 * 128)

    loads = [
        pltpu.make_async_copy(src, dst, lsem.at[i])
        for i, (src, dst) in enumerate(
            [(sizes_hbm, sizes_ref), (rs_hbm, rs_ref), (basis_hbm, basis_ref), (pts_hbm, pts_ref), (skel_hbm, skel_ref),
             (near_hbm, near_ref), (count_hbm, count_ref), (mask_hbm, mask_ref)]
        )
    ]
    for load in loads:
        load.start()

    core, z, x, yl = lax.rem(g, 2), lax.rem(g // 2, 8), lax.rem(g // 16, 4), g // 64
    low = {(dz, dc): lax.rem(z + dz, 8) * 2 + lax.rem(core + dc, 2) for dz in range(8) for dc in range(2)}
    high = {(dx, dy): lax.rem(yl + dy, 2) * 64 + lax.rem(x + dx, 4) * 16 for dx in range(4) for dy in range(2)}
    me = core * 64 + g // 2
    others = [high[s[0], s[1]] + low[s[2], s[3]] for s in OTHERS]
    tiles = [lax.rem(t + d, 4) for d in (2, 1, 3)]
    left, right = lax.rem(g + 127, 128), lax.rem(g + 1, 128)

    barrier = pltpu.get_barrier_semaphore()
    for tt in tiles:
        for gg in (left, right, g):
            pl.semaphore_signal(barrier, inc=1, device_id=(gg, tt), device_id_type=MESH)
    for gg in others:
        pl.semaphore_signal(barrier, inc=1, device_id=(gg, t), device_id_type=MESH)

    loads[0].wait()
    loads[1].wait()
    col = lax.broadcasted_iota(jnp.int32, (1, 128), 1) + t * 128
    live_row = jnp.concatenate([(col < sizes_ref[a]).astype(f32) for a in range(4)], axis=0)
    s_row = live_row * rs_ref[...]
    own_half = lax.rem(t, 2)
    goal_half = t // 2
    lane = lax.broadcasted_iota(jnp.int32, (128, 128), 1)

    def columns(rows):
        return jnp.concatenate(rows + [jnp.zeros((128 - sum(r.shape[0] for r in rows), 128), f32)], axis=0).T

    def spread(cols, i):
        return jnp.broadcast_to(cols[:, i : i + 1], (128, 128))

    cols = columns([s_row, live_row])
    loads[2].wait()
    part_lo = jnp.zeros((128, 128), f32)
    part_hi = jnp.zeros((128, 128), f32)
    s_sq = jnp.zeros((128, 128), f32)
    for a in range(4):
        s_b = spread(cols, a)
        scol[a] = s_b
        s_sq = s_sq + s_b * s_b
        live_col[a] = spread(cols, 4 + a)
        part_lo = part_lo + basis_ref[a, :, :128] * s_b
        part_hi = part_hi + basis_ref[a, :, 128:] * s_b
    abuf[t, 0:1] = jnp.sum(part_lo, axis=0, keepdims=True)
    abuf[t, 1:2] = jnp.sum(part_hi, axis=0, keepdims=True)
    abuf[t, 2:3] = jnp.sum(s_sq, axis=0, keepdims=True)
    abuf[t, 3:4] = jnp.zeros((1, 128), f32)
    for load in loads[3:]:
        load.wait()
    for a in range(4):
        hal1[4 + t, a] = jnp.concatenate([pts_ref[c, a : a + 1, :] for c in range(3)] + [s_row[a : a + 1]], axis=0)
    sk_lo = jnp.concatenate([skel_ref[c, :, :128] for c in range(3)], axis=0)
    sk_hi = jnp.concatenate([skel_ref[c, :, 128:] for c in range(3)], axis=0)
    goals = jnp.where(goal_half == 0, sk_lo, sk_hi)
    skb[me, 0:3] = jnp.where(own_half == 0, sk_lo, sk_hi)

    points_of = basis_ref[...].reshape(512, 256)
    masked = points_of * live_col[...].reshape(512, 128)[:, 0:1]

    def product(left, right):
        return lax.dot_general(
            left, right, (((0,), (0,)), ((), ())), precision=lax.Precision.HIGHEST, preferred_element_type=f32
        )

    upper = product(masked[:, :128], points_of)
    lower = product(masked[:, 128:], points_of[:, 128:])
    mix_own[0] = upper[0:96, :128]
    mix_own[1, 0:32] = upper[96:128, :128]
    mix_own[1, 32:96] = upper[0:64, 128:]
    mix_own[2, 0:64] = upper[64:128, 128:]
    mix_own[2, 64:96] = lower[0:32]
    mix_own[3] = lower[32:128]
    pl.semaphore_wait(barrier, 127 + 9)

    def send(src, dst, which, dev):
        pltpu.make_async_remote_copy(
            src_ref=src, dst_ref=dst, send_sem=ssem.at[which], recv_sem=rsem.at[which], device_id=dev, device_id_type=MESH
        ).start()

    def wait(ref, which):
        pltpu.make_async_copy(ref, ref, rsem.at[which]).wait()

    def drain(ref, which):
        pltpu.make_async_copy(ref, ref, ssem.at[which]).wait()

    def to_tiles(buf, which):
        for tt in tiles:
            send(buf.at[t], buf.at[t], which, (g, tt))

    def to_others(buf, which):
        for gg in others:
            send(buf.at[g], buf.at[g], which, (gg, t))

    def to_halo(buf, which):
        for tt in tiles:
            send(buf.at[4 + t], buf.at[8 + t], which, (left, tt))
            send(buf.at[4 + t], buf.at[t], which, (right, tt))
            send(buf.at[4 + t], buf.at[4 + t], which, (g, tt))
        send(buf.at[4 + t], buf.at[8 + t], which, (left, t))
        send(buf.at[4 + t], buf.at[t], which, (right, t))

    def neighbour(a, slot):
        rel = jnp.clip(lax.rem(near_ref[a, slot] - 4 * g + (4 + 512), 512), 0, 11)
        return rel // 4, lax.rem(rel, 4)

    def kernel_values(base, first, src):
        x, y, z = src[0:1], src[1:2], src[2:3]
        size = x * x + y * y + z * z + spread_sq
        return lax.rsqrt((base[first] + size) + (base[first + 1] * x + base[first + 2] * y + base[first + 3] * z))

    def near_apply(field, visit):
        for a in range(4):
            def body(slot, acc, a=a):
                gg, leaf = neighbour(a, slot)
                weight = jnp.where(slot < count_ref[a], near_scale, 0.0)
                for tt in range(4):
                    values, source = visit(a, slot, tt, gg * 4 + tt, leaf)
                    acc = acc + values * (source * weight)
                return acc

            acc = lax.fori_loop(0, 4, body, jnp.zeros((128, 128), f32), unroll=4)
            ucol[a] = live_col[a] * (field[a] + jnp.sum(acc, axis=1, keepdims=True))

    def near_first():
        def visit(a, slot, tt, place, leaf):
            src = hal1[place, leaf]
            values = kernel_values(tnear, a * 4, src)
            gnear[a * 16 + slot * 4 + tt] = values
            return values, src[3:4]

        near_apply(scol, visit)

    def near_second():
        near_apply(acol, lambda a, slot, tt, place, leaf: (gnear[a * 16 + slot * 4 + tt], hal2[place, leaf]))

    def far_values(side):
        def body(b, carry):
            gfar[2 * b + side] = kernel_values(tfar, 0, skb[64 * side + b])
            return carry

        lax.fori_loop(0, 64, body, 0, unroll=4)

    def far_apply(n):
        def body(b, acc):
            weight = jnp.where(mask_ref[0, b] != 0, far_scale, 0.0)
            return acc + gfar[b] * (cbuf[n, b] * weight)

        acc = lax.fori_loop(0, 128, body, jnp.zeros((128, 128), f32), unroll=8)
        return jnp.sum(acc.T, axis=0, keepdims=True)

    def near_parts(n, fields):
        lo = jnp.zeros((128, 128), f32)
        hi = jnp.zeros((128, 128), f32)
        prods = [jnp.zeros((128, 128), f32) for _ in range(len(fields) + 1)]
        for a in range(4):
            u = ucol[a]
            lo = lo + basis_ref[a, :, :128] * u
            hi = hi + basis_ref[a, :, 128:] * u
            for i, field in enumerate(fields + [ucol]):
                prods[i] = prods[i] + field[a] * u
        pbuf[n, t, 1:2] = jnp.sum(lo, axis=0, keepdims=True)
        pbuf[n, t, 2:3] = jnp.sum(hi, axis=0, keepdims=True)
        packed = jnp.zeros((1, 128), f32)
        for i, prod in enumerate(prods):
            packed = jnp.where(lane[0:1] == i, jnp.sum(prod, axis=0, keepdims=True), packed)
        pbuf[n, t, 3:4] = packed

    def gathered(n):
        low, high = pbuf[n, 0] + pbuf[n, 1], pbuf[n, 2] + pbuf[n, 3]
        both = low + high
        return low[0:1], high[0:1], both[1:2], both[2:3], both[3:4]

    def mixed(sky_lo, sky_hi):
        pair = columns([sky_lo, sky_hi])
        col_lo, col_hi = spread(pair, 0), spread(pair, 1)
        lo = mix[0] * col_lo + mix[1] * col_hi
        hi = mix[2] * col_lo + mix[3] * col_hi
        return jnp.sum(lo, axis=0, keepdims=True), jnp.sum(hi, axis=0, keepdims=True)

    def image(sky_lo, sky_hi, keep):
        rows = jnp.zeros((128, 128), f32)
        for a in range(4):
            far = basis_ref[a, :, :128] * sky_lo + basis_ref[a, :, 128:] * sky_hi
            value = ucol[a] + live_col[a] * jnp.sum(far, axis=1, keepdims=True)
            rows = jnp.where(lane == a, value, rows)
            if keep:
                acol[a] = value
        return rows.T[0:4]

    to_tiles(abuf, COEF)
    to_halo(hal1, HALO_ONE)
    for step, gg in zip(OTHERS, others):
        if step[3] == 0:
            send(skb.at[me, pl.ds(0, 3)], skb.at[me, pl.ds(0, 3)], SKEL, (gg, t))
    for tt in tiles:
        send(mix_own.at[tt], mix_part.at[t], MIX_PART, (g, tt))
    mix_part[t] = mix_own[t]

    goal_rows = [goals[c : c + 1] for c in range(3)]
    cols = columns(
        [-2.0 * pts_ref[c] for c in range(3)] + [sum(pts_ref[c] * pts_ref[c] for c in range(3))]
        + [-2.0 * row for row in goal_rows] + [sum(row * row for row in goal_rows)]
    )
    for c in range(4):
        tfar[(c + 1) % 4] = spread(cols, 16 + c)
        for a in range(4):
            tnear[a * 4 + (c + 1) % 4] = spread(cols, c * 4 + a)

    wait(abuf.at[pl.ds(0, 3)], COEF)
    parts = abuf[0] + abuf[1] + abuf[2] + abuf[3]
    one_lo, one_hi, ss = parts[0:1], parts[1:2], parts[2:3]
    cbuf[0, g] = jnp.where(own_half == 0, one_lo, one_hi)
    to_others(cbuf.at[0], FAR_ONE)
    wait(hal1.at[pl.ds(0, 11)], HALO_ONE)
    near_first()
    wait(skb.at[pl.ds(0, 63), pl.ds(0, 3)], SKEL)
    half = skb.at[pl.ds(core * 64, 64), pl.ds(0, 3)]
    send(half, half, SKEL_PAIR, (g + 1 - 2 * core, t))
    wait(mix_part.at[pl.ds(0, 3)], MIX_PART)
    mix_all[t] = mix_part[0] + mix_part[1] + mix_part[2] + mix_part[3]
    to_tiles(mix_all, MIX_ALL)
    near_parts(0, [scol])
    far_values(core)
    wait(skb.at[pl.ds(0, 64), pl.ds(0, 3)], SKEL_PAIR)
    far_values(1 - core)
    wait(cbuf.at[0, pl.ds(0, 127)], FAR_ONE)
    pbuf[0, t, 0:1] = far_apply(0)
    to_tiles(pbuf.at[0], SKY_ONE)
    wait(mix_all.at[pl.ds(0, 3)], MIX_ALL)
    cross = jnp.concatenate([mix_all[1, 32:96], mix_all[2, 0:64]], axis=0)
    mix[0] = jnp.concatenate([mix_all[0], mix_all[1, 0:32]], axis=0)
    mix[1] = cross.T
    mix[2] = cross
    mix[3] = jnp.concatenate([mix_all[2, 64:96], mix_all[3]], axis=0)
    wait(pbuf.at[0, pl.ds(0, 3)], SKY_ONE)
    sky1_lo, sky1_hi, r1_lo, r1_hi, dots1 = gathered(0)
    a_row = image(sky1_lo, sky1_hi, True)

    for a in range(4):
        hal2[4 + t, a] = a_row[a : a + 1]
    to_halo(hal2, HALO_TWO)
    m1_lo, m1_hi = mixed(sky1_lo, sky1_hi)
    two_lo, two_hi = r1_lo + m1_lo, r1_hi + m1_hi
    cbuf[1, g] = jnp.where(own_half == 0, two_lo, two_hi)
    to_others(cbuf.at[1], FAR_TWO)
    wait(hal2.at[pl.ds(0, 11)], HALO_TWO)
    near_second()
    near_parts(1, [scol, acol])
    wait(cbuf.at[1, pl.ds(0, 127)], FAR_TWO)
    pbuf[1, t, 0:1] = far_apply(1)
    to_tiles(pbuf.at[1], SKY_TWO)
    wait(pbuf.at[1, pl.ds(0, 3)], SKY_TWO)
    sky2_lo, sky2_hi, r2_lo, r2_hi, dots2 = gathered(1)

    m2_lo, m2_hi = mixed(sky2_lo, sky2_hi)
    rows = [
        one_lo * sky1_lo + one_hi * sky1_hi,
        one_lo * sky2_lo + one_hi * sky2_hi,
        (r1_lo + two_lo) * sky1_lo + (r1_hi + two_hi) * sky1_hi,
        two_lo * sky2_lo + two_hi * sky2_hi,
        (2.0 * r2_lo + m2_lo) * sky2_lo + (2.0 * r2_hi + m2_hi) * sky2_hi,
    ]
    near_part = [dots1[:, 0:1], dots2[:, 0:1], dots1[:, 1:2], dots2[:, 1:2], dots2[:, 2:3]]
    far_part = jnp.sum(jnp.concatenate(rows + [jnp.zeros((3, 128), f32)], axis=0), axis=1, keepdims=True)
    packed = ss
    for i in range(5):
        packed = jnp.where(lane[0:1] == i + 1, near_part[i] + far_part[i : i + 1], packed)
    rblk[g] = packed
    to_others(rblk, SUMS)
    b_row = image(sky2_lo, sky2_hi, False)
    wait(rblk.at[pl.ds(0, 127)], SUMS)
    dots = jnp.sum(rblk[...], axis=0)
    ss, sa, sb, aa, ab, bb = [dots[:, i : i + 1] for i in range(6)]

    beta_sq = ss + norm_eps
    beta = jnp.sqrt(beta_sq)
    h11 = sa / beta_sq
    h21_sq = jnp.maximum((aa - 2.0 * h11 * sa + h11 * h11 * ss) / beta_sq, 0.0) + norm_eps
    h21 = jnp.sqrt(h21_sq)
    h12 = (sb - h11 * sa) / (beta_sq * h21)
    h22 = (ab - h11 * aa - h11 * sb + h11 * h11 * sa) / (beta_sq * h21_sq)
    w_sq = (bb - 2.0 * h11 * ab + h11 * h11 * aa) / (beta_sq * h21_sq)
    first_sq = ss / beta_sq
    second_sq = (h21_sq - norm_eps) / h21_sq
    cross_sq = h11 * (1.0 - first_sq) / h21
    rest_sq = w_sq - h12 * h12 * (2.0 - first_sq) - h22 * h22 * (2.0 - second_sq) + 2.0 * h12 * h22 * cross_sq
    h32_sq = jnp.maximum(rest_sq, 0.0) + norm_eps
    m_aa = h11 * h11 + h21_sq
    m_ab = h11 * h12 + h21 * h22
    m_bb = h12 * h12 + h22 * h22 + h32_sq
    determ = m_aa * m_bb - m_ab * m_ab
    y_one = beta * (m_bb * h11 - m_ab * h12) / determ
    y_two = beta * (m_aa * h12 - m_ab * h11) / determ
    c_one = y_one / beta
    c_two = y_two / (beta * h21)
    out_ref[0:4] = c_one * s_row + c_two * (a_row - h11 * s_row)
    out_ref[4:8] = s_row - c_one * a_row - c_two * (b_row - h11 * a_row)

    drain(hal1.at[pl.ds(0, 11)], HALO_ONE)
    drain(hal2.at[pl.ds(0, 11)], HALO_TWO)
    drain(abuf.at[pl.ds(0, 3)], COEF)
    drain(mix_part.at[pl.ds(0, 3)], MIX_PART)
    drain(mix_all.at[pl.ds(0, 3)], MIX_ALL)
    drain(skb.at[pl.ds(0, 63), pl.ds(0, 3)], SKEL)
    drain(skb.at[pl.ds(0, 64), pl.ds(0, 3)], SKEL_PAIR)
    drain(cbuf.at[0, pl.ds(0, 127)], FAR_ONE)
    drain(cbuf.at[1, pl.ds(0, 127)], FAR_TWO)
    drain(pbuf.at[0, pl.ds(0, 3)], SKY_ONE)
    drain(pbuf.at[1, pl.ds(0, 3)], SKY_TWO)
    drain(rblk.at[pl.ds(0, 127)], SUMS)


def per_device(right_side, points, basis, skeleton, cluster_sizes, near_list, near_count, far_mask):
    vmem = pl.BlockSpec(memory_space=pltpu.VMEM)
    hbm = pl.BlockSpec(memory_space=pltpu.HBM)
    both = pl.pallas_call(
        kernel,
        out_shape=jax.ShapeDtypeStruct((8, 128), f32),
        in_specs=[hbm] * 8,
        out_specs=vmem,
        scratch_shapes=[
            pltpu.VMEM((4, 128), f32),
            pltpu.VMEM((3, 4, 128), f32),
            pltpu.VMEM((4, 128, 256), f32),
            pltpu.VMEM((3, 1, 256), f32),
            pltpu.SMEM((4,), jnp.int32),
            pltpu.SMEM((4, 4), jnp.int32),
            pltpu.SMEM((4,), jnp.int32),
            pltpu.SMEM((1, 128), jnp.int32),
            pltpu.VMEM((12, 4, 4, 128), f32),
            pltpu.VMEM((12, 4, 1, 128), f32),
            pltpu.VMEM((4, 4, 128), f32),
            pltpu.VMEM((128, 4, 128), f32),
            pltpu.VMEM((2, 128, 1, 128), f32),
            pltpu.VMEM((2, 4, 4, 128), f32),
            pltpu.VMEM((128, 1, 128), f32),
            pltpu.VMEM((4, 96, 128), f32),
            pltpu.VMEM((4, 96, 128), f32),
            pltpu.VMEM((4, 96, 128), f32),
            pltpu.VMEM((4, 128, 128), f32),
            pltpu.VMEM((128, 128, 128), f32),
            pltpu.VMEM((64, 128, 128), f32),
            pltpu.VMEM((4, 128, 128), f32),
            pltpu.VMEM((16, 128, 128), f32),
            pltpu.VMEM((4, 128, 128), f32),
            pltpu.VMEM((4, 128, 128), f32),
            pltpu.VMEM((4, 128, 128), f32),
            pltpu.VMEM((4, 128, 128), f32),
            pltpu.SemaphoreType.DMA((EXCHANGES,)),
            pltpu.SemaphoreType.DMA((EXCHANGES,)),
            pltpu.SemaphoreType.DMA((8,)),
        ],
        compiler_params=pltpu.CompilerParams(collective_id=0, has_side_effects=True, vmem_limit_bytes=64 * 2**20),
    )(right_side, points, basis, skeleton.transpose(1, 0, 2), cluster_sizes, near_list, near_count, far_mask)
    return both[0:4], both[4:8]


def solution(mesh):
    placed = (
        P("blk", "tile"),
        P(None, "blk", "tile"),
        P("blk", "tile", None),
        P("blk", None, None),
        P("blk"),
        P("blk", None),
        P("blk"),
        P("blk", None),
    )
    return jax.shard_map(
        per_device,
        mesh=mesh,
        in_specs=placed,
        out_specs=(P("blk", "tile"), P("blk", "tile")),
        check_vma=False,
    )
```

```python
import functools
import math

import jax
import jax.numpy as jnp
from jax import lax
from jax.experimental import pallas as pl
from jax.experimental.pallas import tpu as pltpu
from jax.sharding import PartitionSpec as P

MESH = pl.DeviceIdType.MESH
f32 = jnp.float32
spread_sq = 0.25
norm_eps = 1e-06

HALO_ONE, HALO_TWO, COEF, SKEL, SKEL_PAIR, FAR_ONE, FAR_TWO, SKY_ONE, SKY_TWO, MIX_PART, MIX_ALL, SUMS = range(12)
EXCHANGES = 12


def hops(step):
    dx, dyl, dz, dc = step
    return min(dx, 4 - dx) + dyl + min(dz, 8 - dz)


OTHERS = sorted(
    [(dx, dyl, dz, dc) for dx in range(4) for dyl in range(2) for dz in range(8) for dc in range(2) if dx or dyl or dz or dc],
    key=lambda step: -hops(step),
)

FAR = 12


def kernel(
    rs_hbm, pts_hbm, basis_hbm, skel_hbm, sizes_hbm, near_hbm, count_hbm, mask_hbm,
    out_ref,
    rs_ref, pts_ref, basis_ref, skel_ref, sizes_ref, near_ref, count_ref, mask_ref,
    hal1, hal2, abuf, skb, cbuf, pbuf, rblk, mix_own, mix_part, mix_all, mix,
    gfar, gnear, tfar, tnear, scol, ucol, acol, live_col,
    ssem, rsem, lsem,
):
    g = lax.axis_index("blk")
    t = lax.axis_index("tile")
    near_scale = 2.0 / math.sqrt(512 * 4)
    far_scale = 4.0 / math.sqrt(256 * 128)

    loads = [
        pltpu.make_async_copy(src, dst, lsem.at[i])
        for i, (src, dst) in enumerate(
            [(sizes_hbm, sizes_ref), (rs_hbm, rs_ref), (basis_hbm, basis_ref), (pts_hbm, pts_ref), (skel_hbm, skel_ref),
             (near_hbm, near_ref), (count_hbm, count_ref), (mask_hbm, mask_ref)]
        )
    ]
    core, z, x, yl = lax.rem(g, 2), lax.rem(g // 2, 8), lax.rem(g // 16, 4), g // 64
    low = {(dz, dc): lax.rem(z + dz, 8) * 2 + lax.rem(core + dc, 2) for dz in range(8) for dc in range(2)}
    high = {(dx, dy): lax.rem(yl + dy, 2) * 64 + lax.rem(x + dx, 4) * 16 for dx in range(4) for dy in range(2)}
    me = core * 64 + g // 2
    others = [high[s[0], s[1]] + low[s[2], s[3]] for s in OTHERS]
    tiles = [lax.rem(t + d, 4) for d in (2, 1, 3)]
    left, right = lax.rem(g + 127, 128), lax.rem(g + 1, 128)

    barrier = pltpu.get_barrier_semaphore()
    for gg in others[:FAR]:
        pl.semaphore_signal(barrier, inc=1, device_id=(gg, t), device_id_type=MESH)
    for tt in tiles:
        for gg in (left, right, g):
            pl.semaphore_signal(barrier, inc=1, device_id=(gg, tt), device_id_type=MESH)
    for load in loads:
        load.start()
    for gg in others[FAR:]:
        pl.semaphore_signal(barrier, inc=1, device_id=(gg, t), device_id_type=MESH)

    loads[0].wait()
    loads[1].wait()
    col = lax.broadcasted_iota(jnp.int32, (1, 128), 1) + t * 128
    live_row = jnp.concatenate([(col < sizes_ref[a]).astype(f32) for a in range(4)], axis=0)
    s_row = live_row * rs_ref[...]
    own_half = lax.rem(t, 2)
    goal_half = t // 2
    lane = lax.broadcasted_iota(jnp.int32, (128, 128), 1)

    def columns(rows):
        return jnp.concatenate(rows + [jnp.zeros((128 - sum(r.shape[0] for r in rows), 128), f32)], axis=0).T

    def spread(cols, i):
        return jnp.broadcast_to(cols[:, i : i + 1], (128, 128))

    cols = columns([s_row, live_row])
    loads[2].wait()
    part_lo = jnp.zeros((128, 128), f32)
    part_hi = jnp.zeros((128, 128), f32)
    s_sq = jnp.zeros((128, 128), f32)
    for a in range(4):
        s_b = spread(cols, a)
        scol[a] = s_b
        s_sq = s_sq + s_b * s_b
        live_col[a] = spread(cols, 4 + a)
        part_lo = part_lo + basis_ref[a, :, :128] * s_b
        part_hi = part_hi + basis_ref[a, :, 128:] * s_b
    abuf[t, 0:1] = jnp.sum(part_lo, axis=0, keepdims=True)
    abuf[t, 1:2] = jnp.sum(part_hi, axis=0, keepdims=True)
    abuf[t, 2:3] = jnp.sum(s_sq, axis=0, keepdims=True)
    abuf[t, 3:4] = jnp.zeros((1, 128), f32)
    for load in loads[3:]:
        load.wait()
    for a in range(4):
        hal1[4 + t, a] = jnp.concatenate([pts_ref[c, a : a + 1, :] for c in range(3)] + [s_row[a : a + 1]], axis=0)
    sk_lo = jnp.concatenate([skel_ref[c, :, :128] for c in range(3)], axis=0)
    sk_hi = jnp.concatenate([skel_ref[c, :, 128:] for c in range(3)], axis=0)
    goals = jnp.where(goal_half == 0, sk_lo, sk_hi)
    skb[me, 0:3] = jnp.where(own_half == 0, sk_lo, sk_hi)

    points_of = basis_ref[...].reshape(512, 256)
    masked = points_of * live_col[...].reshape(512, 128)[:, 0:1]

    def product(left, right):
        return lax.dot_general(
            left, right, (((0,), (0,)), ((), ())), precision=lax.Precision.HIGHEST, preferred_element_type=f32
        )

    upper = product(masked[:, :128], points_of)
    lower = product(masked[:, 128:], points_of[:, 128:])
    mix_own[0] = upper[0:96, :128]
    mix_own[1, 0:32] = upper[96:128, :128]
    mix_own[1, 32:96] = upper[0:64, 128:]
    mix_own[2, 0:64] = upper[64:128, 128:]
    mix_own[2, 64:96] = lower[0:32]
    mix_own[3] = lower[32:128]
    pl.semaphore_wait(barrier, 127 + 9)

    def send(src, dst, which, dev):
        pltpu.make_async_remote_copy(
            src_ref=src, dst_ref=dst, send_sem=ssem.at[which], recv_sem=rsem.at[which], device_id=dev, device_id_type=MESH
        ).start()

    def wait(ref, which):
        pltpu.make_async_copy(ref, ref, rsem.at[which]).wait()

    def drain(ref, which):
        pltpu.make_async_copy(ref, ref, ssem.at[which]).wait()

    def to_tiles(buf, which):
        for tt in tiles:
            send(buf.at[t], buf.at[t], which, (g, tt))

    def to_others(buf, which, goals=others):
        for gg in goals:
            send(buf.at[g], buf.at[g], which, (gg, t))

    def to_halo(buf, which):
        for tt in tiles:
            send(buf.at[4 + t], buf.at[8 + t], which, (left, tt))
            send(buf.at[4 + t], buf.at[t], which, (right, tt))
            send(buf.at[4 + t], buf.at[4 + t], which, (g, tt))
        send(buf.at[4 + t], buf.at[8 + t], which, (left, t))
        send(buf.at[4 + t], buf.at[t], which, (right, t))

    def neighbour(a, slot):
        rel = jnp.clip(lax.rem(near_ref[a, slot] - 4 * g + (4 + 512), 512), 0, 11)
        return rel // 4, lax.rem(rel, 4)

    def kernel_values(base, first, src):
        x, y, z = src[0:1], src[1:2], src[2:3]
        size = x * x + y * y + z * z + spread_sq
        return lax.rsqrt((base[first] + size) + (base[first + 1] * x + base[first + 2] * y + base[first + 3] * z))

    def near_apply(field, visit):
        for a in range(4):
            def body(slot, acc, a=a):
                gg, leaf = neighbour(a, slot)
                weight = jnp.where(slot < count_ref[a], near_scale, 0.0)
                for tt in range(4):
                    values, source = visit(a, slot, tt, gg * 4 + tt, leaf)
                    acc = acc + values * (source * weight)
                return acc

            acc = lax.fori_loop(0, 4, body, jnp.zeros((128, 128), f32), unroll=4)
            ucol[a] = live_col[a] * (field[a] + jnp.sum(acc, axis=1, keepdims=True))

    def near_first():
        def visit(a, slot, tt, place, leaf):
            src = hal1[place, leaf]
            values = kernel_values(tnear, a * 4, src)
            gnear[a * 16 + slot * 4 + tt] = values
            return values, src[3:4]

        near_apply(scol, visit)

    def near_second():
        near_apply(acol, lambda a, slot, tt, place, leaf: (gnear[a * 16 + slot * 4 + tt], hal2[place, leaf]))

    def far_values(side):
        def body(b, carry):
            gfar[2 * b + side] = kernel_values(tfar, 0, skb[64 * side + b])
            return carry

        lax.fori_loop(0, 64, body, 0, unroll=8)

    def far_apply(n):
        def body(b, acc):
            weight = jnp.where(mask_ref[0, b] != 0, far_scale, 0.0)
            return acc + gfar[b] * (cbuf[n, b] * weight)

        acc = lax.fori_loop(0, 128, body, jnp.zeros((128, 128), f32), unroll=16)
        return jnp.sum(acc.T, axis=0, keepdims=True)

    def near_parts(n, fields):
        lo = jnp.zeros((128, 128), f32)
        hi = jnp.zeros((128, 128), f32)
        prods = [jnp.zeros((128, 128), f32) for _ in range(len(fields) + 1)]
        for a in range(4):
            u = ucol[a]
            lo = lo + basis_ref[a, :, :128] * u
            hi = hi + basis_ref[a, :, 128:] * u
            for i, field in enumerate(fields + [ucol]):
                prods[i] = prods[i] + field[a] * u
        pbuf[n, t, 1:2] = jnp.sum(lo, axis=0, keepdims=True)
        pbuf[n, t, 2:3] = jnp.sum(hi, axis=0, keepdims=True)
        packed = jnp.zeros((1, 128), f32)
        for i, prod in enumerate(prods):
            packed = jnp.where(lane[0:1] == i, jnp.sum(prod, axis=0, keepdims=True), packed)
        pbuf[n, t, 3:4] = packed

    def gathered(n):
        low, high = pbuf[n, 0] + pbuf[n, 1], pbuf[n, 2] + pbuf[n, 3]
        both = low + high
        return low[0:1], high[0:1], both[1:2], both[2:3], both[3:4]

    def mixed(sky_lo, sky_hi):
        pair = columns([sky_lo, sky_hi])
        col_lo, col_hi = spread(pair, 0), spread(pair, 1)
        lo = mix[0] * col_lo + mix[1] * col_hi
        hi = mix[2] * col_lo + mix[3] * col_hi
        return jnp.sum(lo, axis=0, keepdims=True), jnp.sum(hi, axis=0, keepdims=True)

    def image(sky_lo, sky_hi, keep):
        rows = jnp.zeros((128, 128), f32)
        for a in range(4):
            far = basis_ref[a, :, :128] * sky_lo + basis_ref[a, :, 128:] * sky_hi
            value = ucol[a] + live_col[a] * jnp.sum(far, axis=1, keepdims=True)
            rows = jnp.where(lane == a, value, rows)
            if keep:
                acol[a] = value
        return rows.T[0:4]

    to_tiles(abuf, COEF)
    to_halo(hal1, HALO_ONE)
    for step, gg in zip(OTHERS, others):
        if step[3] == 0:
            send(skb.at[me, pl.ds(0, 3)], skb.at[me, pl.ds(0, 3)], SKEL, (gg, t))
    for tt in tiles:
        send(mix_own.at[tt], mix_part.at[t], MIX_PART, (g, tt))
    mix_part[t] = mix_own[t]

    goal_rows = [goals[c : c + 1] for c in range(3)]
    cols = columns(
        [-2.0 * pts_ref[c] for c in range(3)] + [sum(pts_ref[c] * pts_ref[c] for c in range(3))]
        + [-2.0 * row for row in goal_rows] + [sum(row * row for row in goal_rows)]
    )
    for c in range(4):
        tfar[(c + 1) % 4] = spread(cols, 16 + c)
        for a in range(4):
            tnear[a * 4 + (c + 1) % 4] = spread(cols, c * 4 + a)

    wait(abuf.at[pl.ds(0, 3)], COEF)
    parts = abuf[0] + abuf[1] + abuf[2] + abuf[3]
    one_lo, one_hi, ss = parts[0:1], parts[1:2], parts[2:3]
    cbuf[0, g] = jnp.where(own_half == 0, one_lo, one_hi)
    to_others(cbuf.at[0], FAR_ONE)
    wait(hal1.at[pl.ds(0, 11)], HALO_ONE)
    near_first()
    wait(skb.at[pl.ds(0, 63), pl.ds(0, 3)], SKEL)
    half = skb.at[pl.ds(core * 64, 64), pl.ds(0, 3)]
    send(half, half, SKEL_PAIR, (g + 1 - 2 * core, t))
    wait(mix_part.at[pl.ds(0, 3)], MIX_PART)
    mix_all[t] = mix_part[0] + mix_part[1] + mix_part[2] + mix_part[3]
    to_tiles(mix_all, MIX_ALL)
    near_parts(0, [scol])
    far_values(core)
    wait(skb.at[pl.ds(0, 64), pl.ds(0, 3)], SKEL_PAIR)
    far_values(1 - core)
    wait(cbuf.at[0, pl.ds(0, 127)], FAR_ONE)
    pbuf[0, t, 0:1] = far_apply(0)
    to_tiles(pbuf.at[0], SKY_ONE)
    wait(mix_all.at[pl.ds(0, 3)], MIX_ALL)
    cross = jnp.concatenate([mix_all[1, 32:96], mix_all[2, 0:64]], axis=0)
    mix[0] = jnp.concatenate([mix_all[0], mix_all[1, 0:32]], axis=0)
    mix[1] = cross.T
    mix[2] = cross
    mix[3] = jnp.concatenate([mix_all[2, 64:96], mix_all[3]], axis=0)
    wait(pbuf.at[0, pl.ds(0, 3)], SKY_ONE)
    sky1_lo, sky1_hi, r1_lo, r1_hi, dots1 = gathered(0)

    m1_lo, m1_hi = mixed(sky1_lo, sky1_hi)
    two_lo, two_hi = r1_lo + m1_lo, r1_hi + m1_hi
    cbuf[1, g] = jnp.where(own_half == 0, two_lo, two_hi)
    to_others(cbuf.at[1], FAR_TWO, others[:FAR])
    a_row = image(sky1_lo, sky1_hi, True)
    for a in range(4):
        hal2[4 + t, a] = a_row[a : a + 1]
    to_halo(hal2, HALO_TWO)
    to_others(cbuf.at[1], FAR_TWO, others[FAR:])
    wait(hal2.at[pl.ds(0, 11)], HALO_TWO)
    near_second()
    near_parts(1, [scol, acol])
    wait(cbuf.at[1, pl.ds(0, 127)], FAR_TWO)
    pbuf[1, t, 0:1] = far_apply(1)
    to_tiles(pbuf.at[1], SKY_TWO)
    wait(pbuf.at[1, pl.ds(0, 3)], SKY_TWO)
    sky2_lo, sky2_hi, r2_lo, r2_hi, dots2 = gathered(1)

    m2_lo, m2_hi = mixed(sky2_lo, sky2_hi)
    rows = [
        one_lo * sky1_lo + one_hi * sky1_hi,
        one_lo * sky2_lo + one_hi * sky2_hi,
        (r1_lo + two_lo) * sky1_lo + (r1_hi + two_hi) * sky1_hi,
        two_lo * sky2_lo + two_hi * sky2_hi,
        (2.0 * r2_lo + m2_lo) * sky2_lo + (2.0 * r2_hi + m2_hi) * sky2_hi,
    ]
    near_part = [dots1[:, 0:1], dots2[:, 0:1], dots1[:, 1:2], dots2[:, 1:2], dots2[:, 2:3]]
    far_part = jnp.sum(jnp.concatenate(rows + [jnp.zeros((3, 128), f32)], axis=0), axis=1, keepdims=True)
    packed = ss
    for i in range(5):
        packed = jnp.where(lane[0:1] == i + 1, near_part[i] + far_part[i : i + 1], packed)
    rblk[g] = packed
    to_others(rblk, SUMS)
    b_row = image(sky2_lo, sky2_hi, False)
    wait(rblk.at[pl.ds(0, 127)], SUMS)
    dots = jnp.sum(rblk[...], axis=0)
    ss, sa, sb, aa, ab, bb = [dots[:, i : i + 1] for i in range(6)]

    beta_sq = ss + norm_eps
    beta = jnp.sqrt(beta_sq)
    h11 = sa / beta_sq
    h21_sq = jnp.maximum((aa - 2.0 * h11 * sa + h11 * h11 * ss) / beta_sq, 0.0) + norm_eps
    h21 = jnp.sqrt(h21_sq)
    h12 = (sb - h11 * sa) / (beta_sq * h21)
    h22 = (ab - h11 * aa - h11 * sb + h11 * h11 * sa) / (beta_sq * h21_sq)
    w_sq = (bb - 2.0 * h11 * ab + h11 * h11 * aa) / (beta_sq * h21_sq)
    first_sq = ss / beta_sq
    second_sq = (h21_sq - norm_eps) / h21_sq
    cross_sq = h11 * (1.0 - first_sq) / h21
    rest_sq = w_sq - h12 * h12 * (2.0 - first_sq) - h22 * h22 * (2.0 - second_sq) + 2.0 * h12 * h22 * cross_sq
    h32_sq = jnp.maximum(rest_sq, 0.0) + norm_eps
    m_aa = h11 * h11 + h21_sq
    m_ab = h11 * h12 + h21 * h22
    m_bb = h12 * h12 + h22 * h22 + h32_sq
    determ = m_aa * m_bb - m_ab * m_ab
    y_one = beta * (m_bb * h11 - m_ab * h12) / determ
    y_two = beta * (m_aa * h12 - m_ab * h11) / determ
    c_one = y_one / beta
    c_two = y_two / (beta * h21)
    out_ref[0:4] = c_one * s_row + c_two * (a_row - h11 * s_row)
    out_ref[4:8] = s_row - c_one * a_row - c_two * (b_row - h11 * a_row)

    drain(hal1.at[pl.ds(0, 11)], HALO_ONE)
    drain(hal2.at[pl.ds(0, 11)], HALO_TWO)
    drain(abuf.at[pl.ds(0, 3)], COEF)
    drain(mix_part.at[pl.ds(0, 3)], MIX_PART)
    drain(mix_all.at[pl.ds(0, 3)], MIX_ALL)
    drain(skb.at[pl.ds(0, 63), pl.ds(0, 3)], SKEL)
    drain(skb.at[pl.ds(0, 64), pl.ds(0, 3)], SKEL_PAIR)
    drain(cbuf.at[0, pl.ds(0, 127)], FAR_ONE)
    drain(cbuf.at[1, pl.ds(0, 127)], FAR_TWO)
    drain(pbuf.at[0, pl.ds(0, 3)], SKY_ONE)
    drain(pbuf.at[1, pl.ds(0, 3)], SKY_TWO)
    drain(rblk.at[pl.ds(0, 127)], SUMS)


def per_device(right_side, points, basis, skeleton, cluster_sizes, near_list, near_count, far_mask):
    vmem = pl.BlockSpec(memory_space=pltpu.VMEM)
    hbm = pl.BlockSpec(memory_space=pltpu.HBM)
    both = pl.pallas_call(
        kernel,
        out_shape=jax.ShapeDtypeStruct((8, 128), f32),
        in_specs=[hbm] * 8,
        out_specs=vmem,
        scratch_shapes=[
            pltpu.VMEM((4, 128), f32),
            pltpu.VMEM((3, 4, 128), f32),
            pltpu.VMEM((4, 128, 256), f32),
            pltpu.VMEM((3, 1, 256), f32),
            pltpu.SMEM((4,), jnp.int32),
            pltpu.SMEM((4, 4), jnp.int32),
            pltpu.SMEM((4,), jnp.int32),
            pltpu.SMEM((1, 128), jnp.int32),
            pltpu.VMEM((12, 4, 4, 128), f32),
            pltpu.VMEM((12, 4, 1, 128), f32),
            pltpu.VMEM((4, 4, 128), f32),
            pltpu.VMEM((128, 4, 128), f32),
            pltpu.VMEM((2, 128, 1, 128), f32),
            pltpu.VMEM((2, 4, 4, 128), f32),
            pltpu.VMEM((128, 1, 128), f32),
            pltpu.VMEM((4, 96, 128), f32),
            pltpu.VMEM((4, 96, 128), f32),
            pltpu.VMEM((4, 96, 128), f32),
            pltpu.VMEM((4, 128, 128), f32),
            pltpu.VMEM((128, 128, 128), f32),
            pltpu.VMEM((64, 128, 128), f32),
            pltpu.VMEM((4, 128, 128), f32),
            pltpu.VMEM((16, 128, 128), f32),
            pltpu.VMEM((4, 128, 128), f32),
            pltpu.VMEM((4, 128, 128), f32),
            pltpu.VMEM((4, 128, 128), f32),
            pltpu.VMEM((4, 128, 128), f32),
            pltpu.SemaphoreType.DMA((EXCHANGES,)),
            pltpu.SemaphoreType.DMA((EXCHANGES,)),
            pltpu.SemaphoreType.DMA((8,)),
        ],
        compiler_params=pltpu.CompilerParams(collective_id=0, has_side_effects=True, vmem_limit_bytes=64 * 2**20),
    )(right_side, points, basis, skeleton.transpose(1, 0, 2), cluster_sizes, near_list, near_count, far_mask)
    return both[0:4], both[4:8]


def solution(mesh):
    placed = (
        P("blk", "tile"),
        P(None, "blk", "tile"),
        P("blk", "tile", None),
        P("blk", None, None),
        P("blk"),
        P("blk", None),
        P("blk"),
        P("blk", None),
    )
    return jax.shard_map(
        per_device,
        mesh=mesh,
        in_specs=placed,
        out_specs=(P("blk", "tile"), P("blk", "tile")),
        check_vma=False,
    )
```

```python
import functools
import math

import jax
import jax.numpy as jnp
from jax import lax
from jax.experimental import pallas as pl
from jax.experimental.pallas import tpu as pltpu
from jax.sharding import PartitionSpec as P

MESH = pl.DeviceIdType.MESH
f32 = jnp.float32
spread_sq = 0.25
norm_eps = 1e-06

HALO_ONE, HALO_TWO, COEF, SKEL, SKEL_PAIR, FAR_ONE, FAR_TWO, SKY_ONE, SKY_TWO, MIX_PART, MIX_ALL, SUMS = range(12)
EXCHANGES = 12


def hops(step):
    dx, dyl, dz, dc = step
    return min(dx, 4 - dx) + dyl + min(dz, 8 - dz)


OTHERS = sorted(
    [(dx, dyl, dz, dc) for dx in range(4) for dyl in range(2) for dz in range(8) for dc in range(2) if dx or dyl or dz or dc],
    key=lambda step: -hops(step),
)

FAR = 12


def kernel(
    rs_hbm, pts_hbm, basis_hbm, skel_hbm, sizes_hbm, near_hbm, count_hbm, mask_hbm,
    out_ref,
    rs_ref, pts_ref, basis_ref, skel_ref, sizes_ref, near_ref, count_ref, mask_ref,
    hal1, hal2, abuf, skb, cbuf, pbuf, rblk, mix_own, mix_part, mix_all, mix,
    gfar, gnear, tfar, tnear, scol, ucol, acol, live_col,
    ssem, rsem, lsem,
):
    g = lax.axis_index("blk")
    t = lax.axis_index("tile")
    near_scale = 2.0 / math.sqrt(512 * 4)
    far_scale = 4.0 / math.sqrt(256 * 128)

    loads = [
        pltpu.make_async_copy(src, dst, lsem.at[i])
        for i, (src, dst) in enumerate(
            [(sizes_hbm, sizes_ref), (rs_hbm, rs_ref), (basis_hbm, basis_ref), (pts_hbm, pts_ref), (skel_hbm, skel_ref),
             (near_hbm, near_ref), (count_hbm, count_ref), (mask_hbm, mask_ref)]
        )
    ]
    core, z, x, yl = lax.rem(g, 2), lax.rem(g // 2, 8), lax.rem(g // 16, 4), g // 64
    low = {(dz, dc): lax.rem(z + dz, 8) * 2 + lax.rem(core + dc, 2) for dz in range(8) for dc in range(2)}
    high = {(dx, dy): lax.rem(yl + dy, 2) * 64 + lax.rem(x + dx, 4) * 16 for dx in range(4) for dy in range(2)}
    me = core * 64 + g // 2
    others = [high[s[0], s[1]] + low[s[2], s[3]] for s in OTHERS]
    tiles = [lax.rem(t + d, 4) for d in (2, 1, 3)]
    left, right = lax.rem(g + 127, 128), lax.rem(g + 1, 128)

    barrier = pltpu.get_barrier_semaphore()
    for gg in others[:FAR]:
        pl.semaphore_signal(barrier, inc=1, device_id=(gg, t), device_id_type=MESH)
    for tt in tiles:
        for gg in (left, right, g):
            pl.semaphore_signal(barrier, inc=1, device_id=(gg, tt), device_id_type=MESH)
    for load in loads:
        load.start()
    for gg in others[FAR:]:
        pl.semaphore_signal(barrier, inc=1, device_id=(gg, t), device_id_type=MESH)

    loads[0].wait()
    loads[1].wait()
    col = lax.broadcasted_iota(jnp.int32, (1, 128), 1) + t * 128
    live_row = jnp.concatenate([(col < sizes_ref[a]).astype(f32) for a in range(4)], axis=0)
    s_row = live_row * rs_ref[...]
    own_half = lax.rem(t, 2)
    goal_half = t // 2
    lane = lax.broadcasted_iota(jnp.int32, (128, 128), 1)

    def columns(rows):
        return jnp.concatenate(rows + [jnp.zeros((128 - sum(r.shape[0] for r in rows), 128), f32)], axis=0).T

    def spread(cols, i):
        return jnp.broadcast_to(cols[:, i : i + 1], (128, 128))

    cols = columns([s_row, live_row])
    loads[2].wait()
    part_lo = jnp.zeros((128, 128), f32)
    part_hi = jnp.zeros((128, 128), f32)
    s_sq = jnp.zeros((128, 128), f32)
    for a in range(4):
        s_b = spread(cols, a)
        scol[a] = s_b
        s_sq = s_sq + s_b * s_b
        live_col[a] = spread(cols, 4 + a)
        part_lo = part_lo + basis_ref[a, :, :128] * s_b
        part_hi = part_hi + basis_ref[a, :, 128:] * s_b
    abuf[t, 0:1] = jnp.sum(part_lo, axis=0, keepdims=True)
    abuf[t, 1:2] = jnp.sum(part_hi, axis=0, keepdims=True)
    abuf[t, 2:3] = jnp.sum(s_sq, axis=0, keepdims=True)
    abuf[t, 3:4] = jnp.zeros((1, 128), f32)
    for load in loads[3:]:
        load.wait()
    for a in range(4):
        hal1[4 + t, a] = jnp.concatenate([pts_ref[c, a : a + 1, :] for c in range(3)] + [s_row[a : a + 1]], axis=0)
    sk_lo = jnp.concatenate([skel_ref[c, :, :128] for c in range(3)], axis=0)
    sk_hi = jnp.concatenate([skel_ref[c, :, 128:] for c in range(3)], axis=0)
    goals = jnp.where(goal_half == 0, sk_lo, sk_hi)
    skb[me, 0:3] = jnp.where(own_half == 0, sk_lo, sk_hi)

    points_of = basis_ref[...].reshape(512, 256)
    masked = points_of * live_col[...].reshape(512, 128)[:, 0:1]

    def product(left, right):
        return lax.dot_general(
            left, right, (((0,), (0,)), ((), ())), precision=lax.Precision.HIGHEST, preferred_element_type=f32
        )

    upper = product(masked[:, :128], points_of)
    lower = product(masked[:, 128:], points_of[:, 128:])
    mix_own[0] = upper[0:96, :128]
    mix_own[1, 0:32] = upper[96:128, :128]
    mix_own[1, 32:96] = upper[0:64, 128:]
    mix_own[2, 0:64] = upper[64:128, 128:]
    mix_own[2, 64:96] = lower[0:32]
    mix_own[3] = lower[32:128]
    pl.semaphore_wait(barrier, 127 + 9)

    def send(src, dst, which, dev):
        pltpu.make_async_remote_copy(
            src_ref=src, dst_ref=dst, send_sem=ssem.at[which], recv_sem=rsem.at[which], device_id=dev, device_id_type=MESH
        ).start()

    def wait(ref, which):
        pltpu.make_async_copy(ref, ref, rsem.at[which]).wait()

    def drain(ref, which):
        pltpu.make_async_copy(ref, ref, ssem.at[which]).wait()

    def to_tiles(buf, which):
        for tt in tiles:
            send(buf.at[t], buf.at[t], which, (g, tt))

    def to_others(buf, which, goals=others):
        for gg in goals:
            send(buf.at[g], buf.at[g], which, (gg, t))

    def to_halo(buf, which):
        for tt in tiles:
            send(buf.at[4 + t], buf.at[8 + t], which, (left, tt))
            send(buf.at[4 + t], buf.at[t], which, (right, tt))
            send(buf.at[4 + t], buf.at[4 + t], which, (g, tt))
        send(buf.at[4 + t], buf.at[8 + t], which, (left, t))
        send(buf.at[4 + t], buf.at[t], which, (right, t))

    def neighbour(a, slot):
        rel = jnp.clip(lax.rem(near_ref[a, slot] - 4 * g + (4 + 512), 512), 0, 11)
        return rel // 4, lax.rem(rel, 4)

    def kernel_values(base, first, src):
        x, y, z = src[0:1], src[1:2], src[2:3]
        size = x * x + y * y + z * z + spread_sq
        return lax.rsqrt((base[first] + size) + (base[first + 1] * x + base[first + 2] * y + base[first + 3] * z))

    def near_apply(field, visit):
        for a in range(4):
            def body(slot, acc, a=a):
                gg, leaf = neighbour(a, slot)
                weight = jnp.where(slot < count_ref[a], near_scale, 0.0)
                for tt in range(4):
                    values, source = visit(a, slot, tt, gg * 4 + tt, leaf)
                    acc = acc + values * (source * weight)
                return acc

            acc = lax.fori_loop(0, 4, body, jnp.zeros((128, 128), f32), unroll=4)
            ucol[a] = live_col[a] * (field[a] + jnp.sum(acc, axis=1, keepdims=True))

    def near_first():
        def visit(a, slot, tt, place, leaf):
            src = hal1[place, leaf]
            values = kernel_values(tnear, a * 4, src)
            gnear[a * 16 + slot * 4 + tt] = values
            return values, src[3:4]

        near_apply(scol, visit)

    def near_second():
        near_apply(acol, lambda a, slot, tt, place, leaf: (gnear[a * 16 + slot * 4 + tt], hal2[place, leaf]))

    def far_values(side):
        def body(b, carry):
            gfar[2 * b + side] = kernel_values(tfar, 0, skb[64 * side + b])
            return carry

        lax.fori_loop(0, 64, body, 0, unroll=8)

    def far_apply(n):
        def body(b, acc):
            weight = jnp.where(mask_ref[0, b] != 0, far_scale, 0.0)
            return acc + gfar[b] * (cbuf[n, b] * weight)

        acc = lax.fori_loop(0, 128, body, jnp.zeros((128, 128), f32), unroll=16)
        return jnp.sum(acc.T, axis=0, keepdims=True)

    def near_parts(n, fields):
        lo = jnp.zeros((128, 128), f32)
        hi = jnp.zeros((128, 128), f32)
        prods = [jnp.zeros((128, 128), f32) for _ in range(len(fields) + 1)]
        for a in range(4):
            u = ucol[a]
            lo = lo + basis_ref[a, :, :128] * u
            hi = hi + basis_ref[a, :, 128:] * u
            for i, field in enumerate(fields + [ucol]):
                prods[i] = prods[i] + field[a] * u
        pbuf[n, t, 1:2] = jnp.sum(lo, axis=0, keepdims=True)
        pbuf[n, t, 2:3] = jnp.sum(hi, axis=0, keepdims=True)
        packed = jnp.zeros((1, 128), f32)
        for i, prod in enumerate(prods):
            packed = jnp.where(lane[0:1] == i, jnp.sum(prod, axis=0, keepdims=True), packed)
        pbuf[n, t, 3:4] = packed

    def gathered(n):
        low, high = pbuf[n, 0] + pbuf[n, 1], pbuf[n, 2] + pbuf[n, 3]
        both = low + high
        return low[0:1], high[0:1], both[1:2], both[2:3], both[3:4]

    def mixed(sky_lo, sky_hi):
        pair = columns([sky_lo, sky_hi])
        col_lo, col_hi = spread(pair, 0), spread(pair, 1)
        lo = mix[0] * col_lo + mix[1] * col_hi
        hi = mix[2] * col_lo + mix[3] * col_hi
        return jnp.sum(lo, axis=0, keepdims=True), jnp.sum(hi, axis=0, keepdims=True)

    def image(sky_lo, sky_hi, keep):
        rows = jnp.zeros((128, 128), f32)
        for a in range(4):
            far = basis_ref[a, :, :128] * sky_lo + basis_ref[a, :, 128:] * sky_hi
            value = ucol[a] + live_col[a] * jnp.sum(far, axis=1, keepdims=True)
            rows = jnp.where(lane == a, value, rows)
            if keep:
                acol[a] = value
        return rows.T[0:4]

    to_tiles(abuf, COEF)
    to_halo(hal1, HALO_ONE)
    for step, gg in zip(OTHERS, others):
        if step[3] == 0:
            send(skb.at[me, pl.ds(0, 3)], skb.at[me, pl.ds(0, 3)], SKEL, (gg, t))
    for tt in tiles:
        send(mix_own.at[tt], mix_part.at[t], MIX_PART, (g, tt))
    mix_part[t] = mix_own[t]

    goal_rows = [goals[c : c + 1] for c in range(3)]
    cols = columns(
        [-2.0 * pts_ref[c] for c in range(3)] + [sum(pts_ref[c] * pts_ref[c] for c in range(3))]
        + [-2.0 * row for row in goal_rows] + [sum(row * row for row in goal_rows)]
    )
    for c in range(4):
        tfar[(c + 1) % 4] = spread(cols, 16 + c)
        for a in range(4):
            tnear[a * 4 + (c + 1) % 4] = spread(cols, c * 4 + a)

    wait(abuf.at[pl.ds(0, 3)], COEF)
    parts = abuf[0] + abuf[1] + abuf[2] + abuf[3]
    one_lo, one_hi, ss = parts[0:1], parts[1:2], parts[2:3]
    cbuf[0, g] = jnp.where(own_half == 0, one_lo, one_hi)
    to_others(cbuf.at[0], FAR_ONE)
    wait(hal1.at[pl.ds(0, 11)], HALO_ONE)
    near_first()
    wait(mix_part.at[pl.ds(0, 3)], MIX_PART)
    mix_all[t] = mix_part[0] + mix_part[1] + mix_part[2] + mix_part[3]
    to_tiles(mix_all, MIX_ALL)
    near_parts(0, [scol])
    wait(skb.at[pl.ds(0, 63), pl.ds(0, 3)], SKEL)
    half = skb.at[pl.ds(core * 64, 64), pl.ds(0, 3)]
    send(half, half, SKEL_PAIR, (g + 1 - 2 * core, t))
    far_values(core)
    wait(skb.at[pl.ds(0, 64), pl.ds(0, 3)], SKEL_PAIR)
    far_values(1 - core)
    wait(cbuf.at[0, pl.ds(0, 127)], FAR_ONE)
    pbuf[0, t, 0:1] = far_apply(0)
    to_tiles(pbuf.at[0], SKY_ONE)
    wait(mix_all.at[pl.ds(0, 3)], MIX_ALL)
    cross = jnp.concatenate([mix_all[1, 32:96], mix_all[2, 0:64]], axis=0)
    mix[0] = jnp.concatenate([mix_all[0], mix_all[1, 0:32]], axis=0)
    mix[1] = cross.T
    mix[2] = cross
    mix[3] = jnp.concatenate([mix_all[2, 64:96], mix_all[3]], axis=0)
    wait(pbuf.at[0, pl.ds(0, 3)], SKY_ONE)
    sky1_lo, sky1_hi, r1_lo, r1_hi, dots1 = gathered(0)

    m1_lo, m1_hi = mixed(sky1_lo, sky1_hi)
    two_lo, two_hi = r1_lo + m1_lo, r1_hi + m1_hi
    cbuf[1, g] = jnp.where(own_half == 0, two_lo, two_hi)
    to_others(cbuf.at[1], FAR_TWO, others[:FAR])
    a_row = image(sky1_lo, sky1_hi, True)
    for a in range(4):
        hal2[4 + t, a] = a_row[a : a + 1]
    to_halo(hal2, HALO_TWO)
    to_others(cbuf.at[1], FAR_TWO, others[FAR:])
    wait(hal2.at[pl.ds(0, 11)], HALO_TWO)
    near_second()
    near_parts(1, [scol, acol])
    wait(cbuf.at[1, pl.ds(0, 127)], FAR_TWO)
    pbuf[1, t, 0:1] = far_apply(1)
    to_tiles(pbuf.at[1], SKY_TWO)
    wait(pbuf.at[1, pl.ds(0, 3)], SKY_TWO)
    sky2_lo, sky2_hi, r2_lo, r2_hi, dots2 = gathered(1)

    m2_lo, m2_hi = mixed(sky2_lo, sky2_hi)
    rows = [
        one_lo * sky1_lo + one_hi * sky1_hi,
        one_lo * sky2_lo + one_hi * sky2_hi,
        (r1_lo + two_lo) * sky1_lo + (r1_hi + two_hi) * sky1_hi,
        two_lo * sky2_lo + two_hi * sky2_hi,
        (2.0 * r2_lo + m2_lo) * sky2_lo + (2.0 * r2_hi + m2_hi) * sky2_hi,
    ]
    near_part = [dots1[:, 0:1], dots2[:, 0:1], dots1[:, 1:2], dots2[:, 1:2], dots2[:, 2:3]]
    far_part = jnp.sum(jnp.concatenate(rows + [jnp.zeros((3, 128), f32)], axis=0), axis=1, keepdims=True)
    packed = ss
    for i in range(5):
        packed = jnp.where(lane[0:1] == i + 1, near_part[i] + far_part[i : i + 1], packed)
    rblk[g] = packed
    to_others(rblk, SUMS)
    b_row = image(sky2_lo, sky2_hi, False)
    wait(rblk.at[pl.ds(0, 127)], SUMS)
    dots = jnp.sum(rblk[...], axis=0)
    ss, sa, sb, aa, ab, bb = [dots[:, i : i + 1] for i in range(6)]

    inv_beta_sq = 1.0 / (ss + norm_eps)
    h11 = sa * inv_beta_sq
    h21_sq = jnp.maximum((aa - 2.0 * h11 * sa + h11 * h11 * ss) * inv_beta_sq, 0.0) + norm_eps
    h21 = jnp.sqrt(h21_sq)
    inv_h21_sq = 1.0 / h21_sq
    inv_h21 = h21 * inv_h21_sq
    h12 = (sb - h11 * sa) * inv_beta_sq * inv_h21
    h22 = (ab - h11 * aa - h11 * sb + h11 * h11 * sa) * inv_beta_sq * inv_h21_sq
    w_sq = (bb - 2.0 * h11 * ab + h11 * h11 * aa) * inv_beta_sq * inv_h21_sq
    first_sq = ss * inv_beta_sq
    second_sq = (h21_sq - norm_eps) * inv_h21_sq
    cross_sq = h11 * (norm_eps * inv_beta_sq) * inv_h21
    rest_sq = w_sq - h12 * h12 * (2.0 - first_sq) - h22 * h22 * (2.0 - second_sq) + 2.0 * h12 * h22 * cross_sq
    h32_sq = jnp.maximum(rest_sq, 0.0) + norm_eps
    m_aa = h11 * h11 + h21_sq
    m_ab = h11 * h12 + h21 * h22
    m_bb = h12 * h12 + h22 * h22 + h32_sq
    inv_determ = 1.0 / (m_aa * m_bb - m_ab * m_ab)
    c_one = (m_bb * h11 - m_ab * h12) * inv_determ
    c_two = (m_aa * h12 - m_ab * h11) * inv_determ * inv_h21
    out_ref[0:4] = c_one * s_row + c_two * (a_row - h11 * s_row)
    out_ref[4:8] = s_row - c_one * a_row - c_two * (b_row - h11 * a_row)

    drain(hal1.at[pl.ds(0, 11)], HALO_ONE)
    drain(hal2.at[pl.ds(0, 11)], HALO_TWO)
    drain(abuf.at[pl.ds(0, 3)], COEF)
    drain(mix_part.at[pl.ds(0, 3)], MIX_PART)
    drain(mix_all.at[pl.ds(0, 3)], MIX_ALL)
    drain(skb.at[pl.ds(0, 63), pl.ds(0, 3)], SKEL)
    drain(skb.at[pl.ds(0, 64), pl.ds(0, 3)], SKEL_PAIR)
    drain(cbuf.at[0, pl.ds(0, 127)], FAR_ONE)
    drain(cbuf.at[1, pl.ds(0, 127)], FAR_TWO)
    drain(pbuf.at[0, pl.ds(0, 3)], SKY_ONE)
    drain(pbuf.at[1, pl.ds(0, 3)], SKY_TWO)
    drain(rblk.at[pl.ds(0, 127)], SUMS)


def per_device(right_side, points, basis, skeleton, cluster_sizes, near_list, near_count, far_mask):
    vmem = pl.BlockSpec(memory_space=pltpu.VMEM)
    hbm = pl.BlockSpec(memory_space=pltpu.HBM)
    both = pl.pallas_call(
        kernel,
        out_shape=jax.ShapeDtypeStruct((8, 128), f32),
        in_specs=[hbm] * 8,
        out_specs=vmem,
        scratch_shapes=[
            pltpu.VMEM((4, 128), f32),
            pltpu.VMEM((3, 4, 128), f32),
            pltpu.VMEM((4, 128, 256), f32),
            pltpu.VMEM((3, 1, 256), f32),
            pltpu.SMEM((4,), jnp.int32),
            pltpu.SMEM((4, 4), jnp.int32),
            pltpu.SMEM((4,), jnp.int32),
            pltpu.SMEM((1, 128), jnp.int32),
            pltpu.VMEM((12, 4, 4, 128), f32),
            pltpu.VMEM((12, 4, 1, 128), f32),
            pltpu.VMEM((4, 4, 128), f32),
            pltpu.VMEM((128, 4, 128), f32),
            pltpu.VMEM((2, 128, 1, 128), f32),
            pltpu.VMEM((2, 4, 4, 128), f32),
            pltpu.VMEM((128, 1, 128), f32),
            pltpu.VMEM((4, 96, 128), f32),
            pltpu.VMEM((4, 96, 128), f32),
            pltpu.VMEM((4, 96, 128), f32),
            pltpu.VMEM((4, 128, 128), f32),
            pltpu.VMEM((128, 128, 128), f32),
            pltpu.VMEM((64, 128, 128), f32),
            pltpu.VMEM((4, 128, 128), f32),
            pltpu.VMEM((16, 128, 128), f32),
            pltpu.VMEM((4, 128, 128), f32),
            pltpu.VMEM((4, 128, 128), f32),
            pltpu.VMEM((4, 128, 128), f32),
            pltpu.VMEM((4, 128, 128), f32),
            pltpu.SemaphoreType.DMA((EXCHANGES,)),
            pltpu.SemaphoreType.DMA((EXCHANGES,)),
            pltpu.SemaphoreType.DMA((8,)),
        ],
        compiler_params=pltpu.CompilerParams(collective_id=0, has_side_effects=True, vmem_limit_bytes=64 * 2**20),
    )(right_side, points, basis, skeleton.transpose(1, 0, 2), cluster_sizes, near_list, near_count, far_mask)
    return both[0:4], both[4:8]


def solution(mesh):
    placed = (
        P("blk", "tile"),
        P(None, "blk", "tile"),
        P("blk", "tile", None),
        P("blk", None, None),
        P("blk"),
        P("blk", None),
        P("blk"),
        P("blk", None),
    )
    return jax.shard_map(
        per_device,
        mesh=mesh,
        in_specs=placed,
        out_specs=(P("blk", "tile"), P("blk", "tile")),
        check_vma=False,
    )
```
